128 devices in a mesh: ingest: 8 (over x, core), list: 16 (over y, z).
Axes of the slice: x: 4, y: 4, z: 4, core: 2. Of those that a mesh axis runs over, the one named last changes fastest.
Arguments:
- vectors: bfloat16 [393216, 768], P(('ingest', 'list')), may hold values from -6 to 6
- list_ids: int32 [1536], P(('ingest', 'list')), may hold values from 0 to 65535, as said below
- code_ids: int32 [393216, 96], P(('ingest', 'list')), may hold values from 0 to 255
- block_counts: int32 [128, 16], P(('ingest', 'list')), may hold values from 0 to 2, as said below
- centroids: bfloat16 [65536, 768], P('list'), may hold values from -6 to 6
- rotation: bfloat16 [768, 768], replicated, may hold values from -0.21875 to 0.21875
Outputs:
- stored_rows: bfloat16 [1048576, 768], P(('ingest', 'list'))
- codebook_sums: float32 [256, 768], P(('ingest', 'list'))
- code_counts: float32 [256, 96], P(('ingest', 'list'))
The draws below stay inside these ranges and needn't reach their ends.
Inputs may be any that keep to these rules, and one draw needn't show every extreme that they name: `list_ids`: on each device at most 2 blocks have lists of one owner (owner = id // 4096); on each index of ingest one owner has exactly 2 blocks of every device of that index. `block_counts`: entry [d, o] is a send allowance: at most the number of blocks of device d whose list has owner o; on each index of ingest, for the owner that has 2 blocks of every device of that index, the entry is 2 on every such device.
All inputs are finite; a program needn't handle non-finite values.
Results may differ from the reference program's by a relative error of at most 0.0051.
Values may be sent and summed in bfloat16 or wider, within the bound.
A program may use at most 128 MiB of HBM per device.

```python
import jax
import jax.numpy as jnp
from jax import lax

M = 96
DSUB = 8
D = 768
KS = 256
LIST_DEV = 4096
LISTS = 65536
BLK = 256
CAP = 2
BDEV = 12
ROWS = 393216
N_INGEST = 8
N_LIST = 16


def owner_table(key):
    device_count = N_INGEST * N_LIST
    hot_owner = jax.random.randint(jax.random.fold_in(key, 11), (N_INGEST,), 0, N_LIST)

    def device_owners(device):
        subkey = jax.random.fold_in(key, device + 100)
        favored = hot_owner[device // N_LIST]
        others = jnp.arange((N_LIST - 1) * CAP, dtype=jnp.int32) // CAP
        others = others + (others >= favored).astype(jnp.int32)
        picked = jax.random.permutation(jax.random.fold_in(subkey, 1), others)[:BDEV - CAP]
        owners = jnp.concatenate([jnp.full((CAP,), favored, jnp.int32), picked])
        return jax.random.permutation(jax.random.fold_in(subkey, 2), owners)
    owners = jax.vmap(device_owners)(jnp.arange(device_count, dtype=jnp.int32))
    device_hot = hot_owner[jnp.arange(device_count, dtype=jnp.int32) // N_LIST]
    return (owners, device_hot)


def draw_list_ids(key, part):
    owners, device_hot = owner_table(key)
    key = jax.random.fold_in(key, 3)
    local_lists = jax.random.randint(key, owners.shape, 0, LIST_DEV)
    return (owners * LIST_DEV + local_lists).reshape(-1).astype(jnp.int32)


def draw_block_counts(key, part):
    owners, device_hot = owner_table(key)
    key = jax.random.fold_in(key, 5)
    matches = (owners[:, :, None] == jnp.arange(N_LIST, dtype=jnp.int32)[None, None, :]).astype(jnp.int32)
    counts = jnp.sum(matches, axis=1).astype(jnp.int32)
    allowance = jax.random.randint(key, counts.shape, 0, CAP + 1).astype(jnp.int32)
    is_hot = jnp.arange(N_LIST, dtype=jnp.int32)[None, :] == device_hot[:, None]
    return jnp.where(is_hot, counts, jnp.minimum(counts, allowance)).astype(jnp.int32)


def touch_ends(drawn, rng, low, high):
    dims = drawn.shape
    place = [jax.random.randint(jax.random.fold_in(rng, axis), (), 0, dims[axis]) for axis in range(len(dims))]
    drawn = drawn.at[tuple(place)].set(low)
    longest = dims.index(max(dims))
    place[longest] = (place[longest] + 1) % dims[longest]
    return drawn.at[tuple(place)].set(high)


def shard_levels(rng, shape, split, least, largest):
    factor_of = 1.0
    for position, shards_of in split:
        draws = jax.random.uniform(jax.random.fold_in(jax.random.fold_in(rng, 6), position), (shards_of,), jnp.float32, least / len(split), largest / len(split))
        factor_of = factor_of * jnp.repeat(jnp.exp(draws), shape[position] // shards_of).reshape((-1,) + (1,) * (len(shape) - 1 - position))
    return factor_of


def noise(key, shape, deviation, bound, pieces=(), kind=jnp.bfloat16):
    factor_of = shard_levels(key, shape, pieces, -0.22, 0.18) if pieces else 1.0
    values = jax.random.normal(key, shape, jnp.float32) * deviation * factor_of
    return jnp.minimum(jnp.maximum(values, -bound), bound).astype(kind)


def setup_inputs(seed: int = 0) -> dict:
    key_of = jax.random.split(jax.random.key(seed), 7)
    vectors = noise(key_of[0], (ROWS, D), 1.0, 6.0, ((0, 128),))
    list_ids = draw_list_ids(jax.random.fold_in(key_of[6], 71), 0)
    code_ids = touch_ends(jax.random.randint(key_of[2], (ROWS, M), 0, KS), jax.random.fold_in(key_of[2], 1), 0, KS - 1).astype(jnp.int32)
    block_counts = draw_block_counts(jax.random.fold_in(key_of[6], 71), 0)
    centroids = noise(key_of[4], (LISTS, D), 1.0, 6.0, ((0, 16),))
    rotation = noise(key_of[5], (D, D), D ** -0.5, 0.21875)
    return dict(vectors=vectors, list_ids=list_ids, code_ids=code_ids, block_counts=block_counts, centroids=centroids, rotation=rotation)


def codebook_terms(encoded_wide, code_rows, keep_rows):
    row_count = encoded_wide.shape[0]
    weighted = (encoded_wide * keep_rows[:, None]).reshape(row_count * M, DSUB)
    segment_ids = (code_rows + jnp.arange(M, dtype=jnp.int32)[None, :] * KS).reshape(row_count * M)
    code_sums = jax.ops.segment_sum(weighted, segment_ids, num_segments=M * KS)
    code_sums = jnp.transpose(code_sums.reshape(M, KS, DSUB), (1, 0, 2)).reshape(KS, M * DSUB)
    weights = jnp.broadcast_to(keep_rows[:, None], (row_count, M)).reshape(row_count * M)
    code_totals = jax.ops.segment_sum(weights, segment_ids, num_segments=M * KS).reshape(M, KS).T
    return code_sums, code_totals


def reference(vectors, list_ids, code_ids, block_counts, centroids, rotation):
    device_count = N_INGEST * N_LIST
    blocks = vectors.reshape(device_count, BDEV, BLK * D)
    code_blocks = code_ids.reshape(device_count, BDEV * BLK, M)
    block_lists = list_ids.reshape(device_count, BDEV)

    def encode_device(totals, slices):
        block_rows, code_rows, own_lists, counts_row = slices
        owner_index = own_lists // LIST_DEV
        onehot = (owner_index[:, None] == jnp.arange(N_LIST, dtype=jnp.int32)[None, :]).astype(jnp.int32)
        block_rank = jnp.sum(jnp.cumsum(onehot, axis=0) * onehot, axis=1) - 1
        count_limit = jnp.sum(onehot * counts_row[None, :], axis=1)
        kept_mask = block_rank < count_limit
        centre_rows = centroids[own_lists].astype(jnp.float32)
        residual = (block_rows.reshape(BDEV, BLK, D).astype(jnp.float32) - centre_rows[:, None, :]).astype(jnp.bfloat16)
        rotated = jnp.dot(residual.reshape(BDEV * BLK, D), rotation, preferred_element_type=jnp.float32)
        encoded = rotated.astype(jnp.bfloat16)
        keep_rows = jnp.repeat(kept_mask.astype(jnp.float32), BLK)
        code_sums, code_totals = codebook_terms(lax.optimization_barrier(encoded).astype(jnp.float32), code_rows, keep_rows)
        slot_index = owner_index * CAP + block_rank
        selected = kept_mask[None, :] & (slot_index[None, :] == jnp.arange(N_LIST * CAP, dtype=jnp.int32)[:, None])
        source_block = jnp.sum(selected.astype(jnp.int32) * jnp.arange(BDEV, dtype=jnp.int32)[None, :], axis=1)
        filled = jnp.any(selected, axis=1)
        encoded_blocks = encoded.reshape(BDEV, BLK * D)
        outgoing = jnp.where(filled[:, None], encoded_blocks[source_block], jnp.zeros((), jnp.bfloat16))
        return (totals[0] + code_sums, totals[1] + code_totals), outgoing

    zero_totals = (jnp.zeros((KS, D), jnp.float32), jnp.zeros((KS, M), jnp.float32))
    (code_sums, code_totals), send_buffers = lax.scan(encode_device, zero_totals, (blocks, code_blocks, block_lists, block_counts))
    send_buffers = send_buffers.reshape(N_INGEST, N_LIST, N_LIST, CAP * BLK * D)
    stored_rows = jnp.swapaxes(send_buffers, 1, 2).reshape(N_INGEST * N_LIST * N_LIST * CAP * BLK, D)
    return stored_rows, code_sums, code_totals
```

```python
import jax
import jax.numpy as jnp
from jax import lax
from jax.experimental import pallas as pl
from jax.experimental.pallas import tpu as pltpu
from jax.sharding import PartitionSpec as P

M = 96
D = 768
KS = 256
LIST_DEV = 4096
BLK = 256
BDEV = 12
ROWS_DEV = BDEV * BLK
N_LIST = 16
N_INGEST = 8
LANES = 128
CHUNKS = D // LANES
WIDE = D + LANES
HI = 64
MESH = pl.DeviceIdType.MESH
F32 = jnp.float32
BF16 = jnp.bfloat16
FAR = (1, 3, 2)


def iota(shape, axis):
    return lax.broadcasted_iota(jnp.int32, shape, axis)


def exchange(
    vec_hbm, lists, codes_hbm, counts, cent_hbm, rot_hbm,
    stored, mid, share,
    vec, codes, cent, rot, stage, landed, ids_out, ids_in, ids_smem, centre_rows, rows_in, table,
    natural, left, right, left_c, right_c, totals, ring_in, ring_sum, part_out, part_in,
    load_sem, smem_sem, s1, r1, s2, r2, out_sem, s_ids, r_ids, s_rows, r_rows, s_ring, r_ring, s_part, r_part,
):
    i = lax.axis_index("ingest")
    j = lax.axis_index("list")
    y = j // 4
    z = j % 4

    def at(dy, dz):
        return ((y + dy) % 4) * 4 + (z + dz) % 4

    loads = [
        pltpu.make_async_copy(vec_hbm, vec, load_sem.at[0]),
        pltpu.make_async_copy(cent_hbm, cent, load_sem.at[1]),
        pltpu.make_async_copy(codes_hbm, codes, load_sem.at[2]),
        pltpu.make_async_copy(rot_hbm, rot, load_sem.at[3]),
    ]
    for load in loads:
        load.start()

    barrier = pltpu.get_barrier_semaphore()
    for o in range(1, N_LIST):
        pl.semaphore_signal(barrier, inc=1, device_id=(i, at(o // 4, o % 4)), device_id_type=MESH)
    for o in range(1, N_INGEST):
        pl.semaphore_signal(barrier, inc=1, device_id=((i + o) % N_INGEST, j), device_id_type=MESH)

    owners = [lists[b] >> 12 for b in range(BDEV)]
    slots = []
    for b in range(BDEV):
        rank = jnp.int32(0)
        for c in range(b):
            rank = rank + jnp.where(owners[c] == owners[b], 1, 0)
        limit = jnp.int32(0)
        for o in range(N_LIST):
            limit = jnp.where(owners[b] == o, counts[0, o], limit)
        slots.append(jnp.where(rank < limit, owners[b] * 2 + rank, -1))
    for b in range(BDEV):
        table[b] = slots[b]

    def source_of(slot):
        block = jnp.int32(0)
        for b in range(1, BDEV):
            block = jnp.where(slots[b] == slot, b, block)
        return block

    def list_of(slot):
        found = jnp.int32(-1)
        for b in range(BDEV):
            found = jnp.where(slots[b] == slot, lists[b] & (LIST_DEV - 1), found)
        return found

    lane8 = iota((8, LANES), 1)
    for o in range(N_LIST):
        owner = at(o // 4, o % 4)
        ids_out[o] = jnp.where(lane8 == 0, list_of(owner * 2), list_of(owner * 2 + 1))
    ids_in[j] = ids_out[0]

    pl.semaphore_wait(barrier, N_LIST - 1 + N_INGEST - 1)

    id_copies = []
    for o in range(1, N_LIST):
        copy = pltpu.make_async_remote_copy(
            src_ref=ids_out.at[o], dst_ref=ids_in.at[j], send_sem=s_ids.at[o], recv_sem=r_ids.at[o],
            device_id=(i, at(o // 4, o % 4)), device_id_type=MESH)
        copy.start()
        id_copies.append(copy)

    loads[0].wait()

    first = {}
    place = 0
    for d in FAR:
        for e in range(4):
            for r in range(2):
                owner = at(e, d) if r == 0 else at(d, e)
                hop = at(0, d) if r == 0 else at(d, 0)
                stage[place] = vec[source_of(owner * 2 + r)]
                if e == 0:
                    copy = pltpu.make_async_remote_copy(
                        src_ref=stage.at[place], dst_ref=landed.at[j * 2 + r], send_sem=s2.at[r, d, 0],
                        recv_sem=r2.at[r, d, 0], device_id=(i, hop), device_id_type=MESH)
                else:
                    copy = pltpu.make_async_remote_copy(
                        src_ref=stage.at[place], dst_ref=mid.at[r, d, e], send_sem=s1.at[r, d, e],
                        recv_sem=r1.at[r, d, e], device_id=(i, hop), device_id_type=MESH)
                copy.start()
                first[r, d, e] = copy
                place += 1

    second = []
    for e in FAR:
        for r in range(2):
            owner = at(e, 0) if r == 0 else at(0, e)
            stage[place] = vec[source_of(owner * 2 + r)]
            copy = pltpu.make_async_remote_copy(
                src_ref=stage.at[place], dst_ref=landed.at[j * 2 + r], send_sem=s2.at[r, 0, e], recv_sem=r2.at[r, 0, e],
                device_id=(i, owner), device_id_type=MESH)
            copy.start()
            second.append(copy)
            place += 1
    for r in range(2):
        landed[j * 2 + r] = vec[source_of(j * 2 + r)]

    for copy in id_copies:
        copy.wait_recv()
    to_smem = pltpu.make_async_copy(ids_in, ids_smem, smem_sem.at[0])
    to_smem.start()
    to_smem.wait()
    loads[1].wait()
    sub16 = iota((16, D), 0)
    pad = jnp.zeros((2, LANES), F32)
    row_copies = []
    for o in range(N_LIST):
        source = at(-(o // 4) % 4, -(o % 4) % 4)
        parts = []
        for r in range(2):
            wanted = jnp.maximum(ids_smem[source, 0, r], 0)
            near = cent[wanted >> 4].astype(F32)
            row = jnp.sum(jnp.where(sub16 == (wanted & 15), near, 0.0), axis=0, keepdims=True)
            parts += [row[:, k * LANES:(k + 1) * LANES] for k in range(CHUNKS)] + [pad]
        centre_rows[source] = jnp.concatenate(parts, axis=0).astype(BF16)
        if o == 0:
            rows_in[j] = centre_rows[source]
        else:
            copy = pltpu.make_async_remote_copy(
                src_ref=centre_rows.at[source], dst_ref=rows_in.at[j], send_sem=s_rows.at[o], recv_sem=r_rows.at[o],
                device_id=(i, source), device_id_type=MESH)
            copy.start()
            row_copies.append(copy)
    loads[2].wait()
    loads[3].wait()
    for copy in row_copies:
        copy.wait_recv()

    eye = (iota((BLK, BLK), 0) == iota((BLK, BLK), 1)).astype(BF16)
    none = jnp.zeros((LANES - M, BLK), F32)

    def rotate(rows, centre):
        residual = jnp.concatenate([
            (rows[:, k * LANES:(k + 1) * LANES].astype(F32) - centre[k:k + 1, :]).astype(BF16) for k in range(CHUNKS)
        ], axis=1)
        return jnp.dot(residual, rot[...], preferred_element_type=F32)

    def encode(b, carry):
        slot = table[b]
        kept = slot >= 0
        slot = jnp.maximum(slot, 0)
        tile = rows_in[slot >> 1].astype(F32)
        centre = jnp.where((slot & 1) == 0, tile[0:8], tile[8:16])
        vec[b] = jnp.where(kept, rotate(vec[b], centre), 0.0).astype(BF16)
        code = codes[:, pl.ds(pl.multiple_of(b * BLK, BLK), BLK)]
        both = jnp.concatenate([
            (code >> 6).astype(F32), none, jnp.where(kept, (code >> 4).astype(F32), -1.0), none], axis=0).astype(BF16)
        natural[b] = lax.dot_general(
            eye, both, (((1,), (1,)), ((), ())), preferred_element_type=F32).astype(BF16)
        return carry

    lax.fori_loop(0, BDEV, encode, 0)

    totals[:, D:] = jnp.zeros((KS, LANES), F32)
    lane = iota((BLK, LANES), 1)
    upper = (lane >= 64).astype(F32)
    lane_r = iota((HI, 2 * LANES), 1)
    lane_c = iota((HI, LANES), 1)
    lane_16 = iota((16, 2 * LANES), 1)
    hi_rows = iota((HI, BLK), 0)
    wide_row = iota((LANES, 2 * LANES), 0)
    wide_lane = iota((LANES, 2 * LANES), 1)
    digit = (iota((BLK, 2 * LANES), 1) // 16).astype(F32)

    def group(g, carry):
        spread = (wide_row == g * 16 + (wide_lane // LANES) * 8 + (wide_lane % 64) // 8).astype(BF16)
        spread_c = (wide_row == g * 16 + wide_lane % 16).astype(BF16)
        cols = pl.ds(pl.multiple_of(g * LANES, LANES), LANES)
        base = pl.multiple_of(g * 16, 16)

        def build(b, inner):
            rows = pl.ds(pl.multiple_of(b * BLK, BLK), BLK)
            lo = jnp.dot(natural[b, :, :LANES], spread, preferred_element_type=F32)
            e = vec[b, :, cols].astype(F32)
            turned = pltpu.roll(e, 64, 1)
            for h in range(2):
                both = jnp.where(lane < 64, e, turned) if h == 0 else jnp.where(lane < 64, turned, e)
                lo_h = lo[:, h * LANES:(h + 1) * LANES]
                for p in range(2):
                    right[h, rows, p * LANES:(p + 1) * LANES] = jnp.where(
                        lo_h == upper + float(2 * p), both, 0.0).astype(BF16)
            high = jnp.dot(natural[b, :, LANES:], spread_c, preferred_element_type=F32)
            right_c[rows, :] = jnp.where(high == digit, 1.0, 0.0).astype(BF16)
            code = codes[pl.ds(base, 16), rows] & 15
            for m in range(16):
                left_c[m * 16:(m + 1) * 16, rows] = jnp.where(
                    code[m:m + 1, :] == hi_rows[:16], 1.0, 0.0).astype(BF16)
            return inner

        lax.fori_loop(0, BDEV, build, 0)
        halves = []
        for h in range(2):

            def build_left(b, inner):
                rows = pl.ds(pl.multiple_of(b * BLK, BLK), BLK)
                code = codes[pl.ds(base + h * 8, 8), rows] & (HI - 1)
                for m in range(8):
                    left[m * HI:(m + 1) * HI, rows] = jnp.where(code[m:m + 1, :] == hi_rows, 1.0, 0.0).astype(BF16)
                return inner

            lax.fori_loop(0, BDEV, build_left, 0)
            sums = jnp.dot(left[...], right[h], preferred_element_type=F32)
            picked = jnp.zeros((HI, 2 * LANES), F32)
            for m in range(8):
                picked = picked + jnp.where((lane_r % 64) // 8 == m, sums[m * HI:(m + 1) * HI, :], 0.0)
            halves.append(picked)
        for p in range(2):
            a = halves[0][:, p * LANES:(p + 1) * LANES]
            c = halves[1][:, p * LANES:(p + 1) * LANES]
            totals[(2 * p) * HI:(2 * p + 1) * HI, cols] = jnp.where(lane_c < 64, a, pltpu.roll(c, 64, 1))
            totals[(2 * p + 1) * HI:(2 * p + 2) * HI, cols] = jnp.where(lane_c < 64, pltpu.roll(a, 64, 1), c)
        found = jnp.dot(left_c[...], right_c[...], preferred_element_type=F32)
        picked = jnp.zeros((16, 2 * LANES), F32)
        for m in range(16):
            picked = picked + jnp.where(lane_16 % 16 == m, found[m * 16:(m + 1) * 16, :], 0.0)
        for q in range(16):
            part = picked[:, (q // 8) * LANES:(q // 8 + 1) * LANES]
            moved = pltpu.roll(part, (g * 16 - (q % 8) * 16) % LANES, 1)
            totals[q * 16:(q + 1) * 16, D:] += jnp.where(lane_c[:16] // 16 == g, moved, 0.0)
        return carry

    lax.fori_loop(0, CHUNKS, group, 0)

    slab = KS // N_INGEST
    ring_copies = []
    for o in range(1, N_INGEST):
        target = (i + o) % N_INGEST
        copy = pltpu.make_async_remote_copy(
            src_ref=totals.at[pl.ds(pl.multiple_of(target * slab, slab), slab), :], dst_ref=ring_in.at[o],
            send_sem=s_ring.at[o], recv_sem=r_ring.at[o], device_id=(target, j), device_id_type=MESH)
        copy.start()
        ring_copies.append(copy)

    for d in FAR:
        for e in FAR:
            for r in range(2):
                owner = at(e, 0) if r == 0 else at(0, e)
                origin = at(0, -d) if r == 0 else at(-d, 0)
                first[r, d, e].wait_recv()
                copy = pltpu.make_async_remote_copy(
                    src_ref=mid.at[r, d, e], dst_ref=landed.at[origin * 2 + r], send_sem=s2.at[r, d, e],
                    recv_sem=r2.at[r, d, e], device_id=(i, owner), device_id_type=MESH)
                copy.start()
                second.append(copy)

    for copy in ring_copies:
        copy.wait_recv()
    whole = totals[pl.ds(pl.multiple_of(i * slab, slab), slab), :]
    for o in range(1, N_INGEST):
        whole = whole + ring_in[o]
    ring_sum[...] = whole
    zero_row = jnp.zeros((1, LANES), F32)
    for o in range(N_LIST):
        target = at(o // 4, o % 4)
        eight = ring_sum[pl.ds(pl.multiple_of((target // 4) * 8, 8), 8), :]
        rows = []
        for r in range(2):
            row = jnp.sum(jnp.where(iota((8, WIDE), 0) == (target % 4) * 2 + r, eight, 0.0), axis=0, keepdims=True)
            rows += [row[:, k * LANES:(k + 1) * LANES] for k in range(CHUNKS + 1)] + [zero_row]
        part_out[o] = jnp.concatenate(rows, axis=0)
    part_copies = []
    for o in range(1, N_LIST):
        copy = pltpu.make_async_remote_copy(
            src_ref=part_out.at[o], dst_ref=part_in.at[o], send_sem=s_part.at[o], recv_sem=r_part.at[o],
            device_id=(i, at(o // 4, o % 4)), device_id_type=MESH)
        copy.start()
        part_copies.append(copy)

    def write_of(slot):
        return pltpu.make_async_copy(landed.at[slot], stored.at[slot], out_sem.at[slot])

    def finish(slot, r):
        source = slot // 2
        centre = centre_rows[source].astype(F32)[r * 8:(r + 1) * 8]
        rotated = rotate(landed[slot], centre)
        landed[slot] = jnp.where(ids_smem[source, 0, r] >= 0, rotated, 0.0).astype(BF16)
        write_of(slot).start()

    def arrival(d, e):
        for r in range(2):
            origin = at(4 - e, 4 - d) if r == 0 else at(4 - d, 4 - e)
            slot = origin * 2 + r
            pltpu.make_async_remote_copy(
                src_ref=stage.at[0], dst_ref=landed.at[slot], send_sem=s2.at[r, d, e], recv_sem=r2.at[r, d, e],
                device_id=(i, origin), device_id_type=MESH).wait_recv()
            finish(slot, r)

    for r in range(2):
        finish(j * 2 + r, r)

    def near_first(t, carry):
        arrival(t + 1, 0)
        return carry

    def near_second(t, carry):
        arrival(0, t + 1)
        return carry

    def far(t, carry):
        arrival(t // 3 + 1, t % 3 + 1)
        return carry

    lax.fori_loop(0, 3, near_first, 0)
    lax.fori_loop(0, 3, near_second, 0)
    for copy in part_copies:
        copy.wait_recv()
    total = part_out[0]
    for o in range(1, N_LIST):
        total = total + part_in[o]
    share[...] = total
    lax.fori_loop(0, 9, far, 0)

    for copy in id_copies + row_copies + ring_copies + part_copies + list(first.values()) + second:
        copy.wait_send()

    def written(slot, carry):
        write_of(slot).wait()
        return carry

    lax.fori_loop(0, 2 * N_LIST, written, 0)


def shards(vectors, list_ids, code_ids, block_counts, centroids, rotation):
    hbm = pl.BlockSpec(memory_space=pl.ANY)
    smem = pl.BlockSpec(memory_space=pltpu.SMEM)
    vmem = pl.BlockSpec(memory_space=pltpu.VMEM)
    dma = pltpu.SemaphoreType.DMA
    stored, _, share = pl.pallas_call(
        exchange,
        out_shape=(
            jax.ShapeDtypeStruct((2 * N_LIST, BLK, D), BF16),
            jax.ShapeDtypeStruct((2, 4, 4, BLK, D), BF16),
            jax.ShapeDtypeStruct((16, LANES), F32),
        ),
        in_specs=[hbm, smem, hbm, smem, hbm, hbm],
        out_specs=(hbm, hbm, vmem),
        scratch_shapes=[
            pltpu.VMEM((BDEV, BLK, D), BF16),
            pltpu.VMEM((M, ROWS_DEV), jnp.int32),
            pltpu.VMEM((LIST_DEV // 16, 16, D), BF16),
            pltpu.VMEM((D, D), BF16),
            pltpu.VMEM((2 * N_LIST - 2, BLK, D), BF16),
            pltpu.VMEM((2 * N_LIST, BLK, D), BF16),
            pltpu.VMEM((N_LIST, 8, LANES), jnp.int32),
            pltpu.VMEM((N_LIST, 8, LANES), jnp.int32),
            pltpu.SMEM((N_LIST, 8, LANES), jnp.int32),
            pltpu.VMEM((N_LIST, 16, LANES), BF16),
            pltpu.VMEM((N_LIST, 16, LANES), BF16),
            pltpu.SMEM((BDEV,), jnp.int32),
            pltpu.VMEM((BDEV, BLK, 2 * LANES), BF16),
            pltpu.VMEM((8 * HI, ROWS_DEV), BF16),
            pltpu.VMEM((2, ROWS_DEV, 2 * LANES), BF16),
            pltpu.VMEM((2 * LANES, ROWS_DEV), BF16),
            pltpu.VMEM((ROWS_DEV, 2 * LANES), BF16),
            pltpu.VMEM((KS, WIDE), F32),
            pltpu.VMEM((N_INGEST, KS // N_INGEST, WIDE), F32),
            pltpu.VMEM((KS // N_INGEST, WIDE), F32),
            pltpu.VMEM((N_LIST, 16, LANES), F32),
            pltpu.VMEM((N_LIST, 16, LANES), F32),
            dma((4,)), dma((1,)),
            dma((2, 4, 4)), dma((2, 4, 4)), dma((2, 4, 4)), dma((2, 4, 4)), dma((2 * N_LIST,)),
            dma((N_LIST,)), dma((N_LIST,)), dma((N_LIST,)), dma((N_LIST,)),
            dma((N_INGEST,)), dma((N_INGEST,)), dma((N_LIST,)), dma((N_LIST,)),
        ],
        compiler_params=pltpu.CompilerParams(
            collective_id=1, has_side_effects=True, vmem_limit_bytes=62 * 1024 * 1024),
        name="exchange",
    )(
        vectors.reshape(BDEV, BLK, D), list_ids, code_ids.T, block_counts,
        centroids.reshape(LIST_DEV // 16, 16, D), rotation,
    )
    parts = share.reshape(2, 8, LANES)
    return stored.reshape(2 * N_LIST * BLK, D), parts[:, :CHUNKS].reshape(2, D), parts[:, CHUNKS, :M]


def solution(mesh):
    both = ("ingest", "list")
    in_specs = (P(both, None), P(both), P(both, None), P(both, None), P("list", None), P())
    out_specs = (P(both, None), P(both, None), P(both, None))
    return jax.shard_map(shards, mesh=mesh, in_specs=in_specs, out_specs=out_specs, check_vma=False)
```

```python
import jax
import jax.numpy as jnp
from jax import lax
from jax.experimental import pallas as pl
from jax.experimental.pallas import tpu as pltpu
from jax.sharding import PartitionSpec as P

M = 96
D = 768
KS = 256
LIST_DEV = 4096
BLK = 256
BDEV = 12
ROWS_DEV = BDEV * BLK
N_LIST = 16
N_INGEST = 8
LANES = 128
CHUNKS = D // LANES
WIDE = D + LANES
HI = 64
MESH = pl.DeviceIdType.MESH
F32 = jnp.float32
BF16 = jnp.bfloat16
FAR = (1, 3, 2)


ORDER = [(d, e, r) for e in (1, 3, 2, 0) for d in (1, 3, 2) for r in range(2)]


def iota(shape, axis):
    return lax.broadcasted_iota(jnp.int32, shape, axis)


def exchange(
    vec_hbm, lists, codes_hbm, counts, cent_hbm, rot_hbm,
    landed, mid, share,
    vec, codes, cent, rot, stage, ids_out, ids_in, ids_smem, centre_rows, rows_in, table,
    natural, left, right, left_c, right_c, totals, ring_in, ring_sum, part_out, part_in,
    load_sem, smem_sem, s1, r1, s2, r2, s_ids, r_ids, s_rows, r_rows, s_ring, r_ring, s_part, r_part,
):
    i = lax.axis_index("ingest")
    j = lax.axis_index("list")
    y = j // 4
    z = j % 4

    def at(dy, dz):
        return ((y + dy) % 4) * 4 + (z + dz) % 4

    loads = [
        pltpu.make_async_copy(vec_hbm, vec, load_sem.at[0]),
        pltpu.make_async_copy(cent_hbm, cent, load_sem.at[1]),
        pltpu.make_async_copy(codes_hbm, codes, load_sem.at[2]),
        pltpu.make_async_copy(rot_hbm, rot, load_sem.at[3]),
    ]
    loads[0].start()

    barrier = pltpu.get_barrier_semaphore()
    for o in range(1, N_LIST):
        pl.semaphore_signal(barrier, inc=1, device_id=(i, at(o // 4, o % 4)), device_id_type=MESH)
    for o in range(1, N_INGEST):
        pl.semaphore_signal(barrier, inc=1, device_id=((i + o) % N_INGEST, j), device_id_type=MESH)

    owners = [lists[b] >> 12 for b in range(BDEV)]
    slots = []
    for b in range(BDEV):
        rank = jnp.int32(0)
        for c in range(b):
            rank = rank + jnp.where(owners[c] == owners[b], 1, 0)
        limit = jnp.int32(0)
        for o in range(N_LIST):
            limit = jnp.where(owners[b] == o, counts[0, o], limit)
        slots.append(jnp.where(rank < limit, owners[b] * 2 + rank, -1))
    for b in range(BDEV):
        table[b] = slots[b]

    def source_of(slot):
        block = jnp.int32(0)
        for b in range(1, BDEV):
            block = jnp.where(slots[b] == slot, b, block)
        return block

    def list_of(slot):
        found = jnp.int32(-1)
        for b in range(BDEV):
            found = jnp.where(slots[b] == slot, lists[b] & (LIST_DEV - 1), found)
        return found

    lane8 = iota((8, LANES), 1)
    for o in range(N_LIST):
        owner = at(o // 4, o % 4)
        ids_out[o] = jnp.where(lane8 == 0, list_of(owner * 2), list_of(owner * 2 + 1))
    ids_in[j] = ids_out[0]

    pl.semaphore_wait(barrier, N_LIST - 1 + N_INGEST - 1)

    id_copies = []
    for o in range(1, N_LIST):
        copy = pltpu.make_async_remote_copy(
            src_ref=ids_out.at[o], dst_ref=ids_in.at[j], send_sem=s_ids.at[o], recv_sem=r_ids.at[o],
            device_id=(i, at(o // 4, o % 4)), device_id_type=MESH)
        copy.start()
        id_copies.append(copy)

    for load in loads[1:]:
        load.start()
    loads[0].wait()

    first = {}
    place = 0
    for d, e, r in ORDER[:4]:
        if True:
            if True:
                owner = at(e, d) if r == 0 else at(d, e)
                hop = at(0, d) if r == 0 else at(d, 0)
                stage[place] = vec[source_of(owner * 2 + r)]
                if e == 0:
                    copy = pltpu.make_async_remote_copy(
                        src_ref=stage.at[place], dst_ref=landed.at[j * 2 + r], send_sem=s2.at[r, d, 0],
                        recv_sem=r2.at[r, d, 0], device_id=(i, hop), device_id_type=MESH)
                else:
                    copy = pltpu.make_async_remote_copy(
                        src_ref=stage.at[place], dst_ref=mid.at[r, d, e], send_sem=s1.at[r, d, e],
                        recv_sem=r1.at[r, d, e], device_id=(i, hop), device_id_type=MESH)
                copy.start()
                first[r, d, e] = copy
                place += 1

    for copy in id_copies:
        copy.wait_recv()
    to_smem = pltpu.make_async_copy(ids_in, ids_smem, smem_sem.at[0])
    to_smem.start()
    to_smem.wait()
    loads[1].wait()
    sub16 = iota((16, D), 0)
    pad = jnp.zeros((2, LANES), F32)
    row_copies = []
    for o in range(N_LIST):
        source = at(-(o // 4) % 4, -(o % 4) % 4)
        parts = []
        for r in range(2):
            wanted = jnp.maximum(ids_smem[source, 0, r], 0)
            near = cent[wanted >> 4].astype(F32)
            row = jnp.sum(jnp.where(sub16 == (wanted & 15), near, 0.0), axis=0, keepdims=True)
            parts += [row[:, k * LANES:(k + 1) * LANES] for k in range(CHUNKS)] + [pad]
        centre_rows[source] = jnp.concatenate(parts, axis=0).astype(BF16)
        if o == 0:
            rows_in[j] = centre_rows[source]
        else:
            copy = pltpu.make_async_remote_copy(
                src_ref=centre_rows.at[source], dst_ref=rows_in.at[j], send_sem=s_rows.at[o], recv_sem=r_rows.at[o],
                device_id=(i, source), device_id_type=MESH)
            copy.start()
            row_copies.append(copy)
    for d, e, r in ORDER[4:]:
        if True:
            if True:
                owner = at(e, d) if r == 0 else at(d, e)
                hop = at(0, d) if r == 0 else at(d, 0)
                stage[place] = vec[source_of(owner * 2 + r)]
                if e == 0:
                    copy = pltpu.make_async_remote_copy(
                        src_ref=stage.at[place], dst_ref=landed.at[j * 2 + r], send_sem=s2.at[r, d, 0],
                        recv_sem=r2.at[r, d, 0], device_id=(i, hop), device_id_type=MESH)
                else:
                    copy = pltpu.make_async_remote_copy(
                        src_ref=stage.at[place], dst_ref=mid.at[r, d, e], send_sem=s1.at[r, d, e],
                        recv_sem=r1.at[r, d, e], device_id=(i, hop), device_id_type=MESH)
                copy.start()
                first[r, d, e] = copy
                place += 1

    second = []
    for e in FAR:
        for r in range(2):
            owner = at(e, 0) if r == 0 else at(0, e)
            stage[place] = vec[source_of(owner * 2 + r)]
            copy = pltpu.make_async_remote_copy(
                src_ref=stage.at[place], dst_ref=landed.at[j * 2 + r], send_sem=s2.at[r, 0, e], recv_sem=r2.at[r, 0, e],
                device_id=(i, owner), device_id_type=MESH)
            copy.start()
            second.append(copy)
            place += 1
    for r in range(2):
        landed[j * 2 + r] = vec[source_of(j * 2 + r)]

    loads[2].wait()
    loads[3].wait()
    for copy in row_copies:
        copy.wait_recv()

    eye = (iota((BLK, BLK), 0) == iota((BLK, BLK), 1)).astype(BF16)
    none = jnp.zeros((LANES - M, BLK), F32)

    def rotate(rows, centre):
        residual = jnp.concatenate([
            (rows[:, k * LANES:(k + 1) * LANES].astype(F32) - centre[k:k + 1, :]).astype(BF16) for k in range(CHUNKS)
        ], axis=1)
        return jnp.dot(residual, rot[...], preferred_element_type=F32)

    def encode(b, carry):
        slot = table[b]
        kept = slot >= 0
        slot = jnp.maximum(slot, 0)
        tile = rows_in[slot >> 1].astype(F32)
        centre = jnp.where((slot & 1) == 0, tile[0:8], tile[8:16])
        vec[b] = jnp.where(kept, rotate(vec[b], centre), 0.0).astype(BF16)
        code = codes[:, pl.ds(pl.multiple_of(b * BLK, BLK), BLK)]
        both = jnp.concatenate([
            (code >> 6).astype(F32), none, jnp.where(kept, (code >> 4).astype(F32), -1.0), none], axis=0).astype(BF16)
        natural[b] = lax.dot_general(
            eye, both, (((1,), (1,)), ((), ())), preferred_element_type=F32).astype(BF16)
        return carry

    lax.fori_loop(0, BDEV, encode, 0)

    totals[:, D:] = jnp.zeros((KS, LANES), F32)
    lane = iota((BLK, LANES), 1)
    upper = (lane >= 64).astype(F32)
    lane_r = iota((HI, 2 * LANES), 1)
    lane_c = iota((HI, LANES), 1)
    lane_16 = iota((16, 2 * LANES), 1)
    hi_rows = iota((HI, BLK), 0)
    wide_row = iota((LANES, 2 * LANES), 0)
    wide_lane = iota((LANES, 2 * LANES), 1)
    digit = (iota((BLK, 2 * LANES), 1) // 16).astype(F32)

    def group(g, carry):
        spread = (wide_row == g * 16 + (wide_lane // LANES) * 8 + (wide_lane % 64) // 8).astype(BF16)
        spread_c = (wide_row == g * 16 + wide_lane % 16).astype(BF16)
        cols = pl.ds(pl.multiple_of(g * LANES, LANES), LANES)
        base = pl.multiple_of(g * 16, 16)

        def build(b, inner):
            rows = pl.ds(pl.multiple_of(b * BLK, BLK), BLK)
            lo = jnp.dot(natural[b, :, :LANES], spread, preferred_element_type=F32)
            e = vec[b, :, cols].astype(F32)
            turned = pltpu.roll(e, 64, 1)
            for h in range(2):
                both = jnp.where(lane < 64, e, turned) if h == 0 else jnp.where(lane < 64, turned, e)
                lo_h = lo[:, h * LANES:(h + 1) * LANES]
                for p in range(2):
                    right[h, rows, p * LANES:(p + 1) * LANES] = jnp.where(
                        lo_h == upper + float(2 * p), both, 0.0).astype(BF16)
            high = jnp.dot(natural[b, :, LANES:], spread_c, preferred_element_type=F32)
            right_c[rows, :] = jnp.where(high == digit, 1.0, 0.0).astype(BF16)
            code = codes[pl.ds(base, 16), rows] & 15
            for m in range(16):
                left_c[m * 16:(m + 1) * 16, rows] = jnp.where(
                    code[m:m + 1, :] == hi_rows[:16], 1.0, 0.0).astype(BF16)
            return inner

        lax.fori_loop(0, BDEV, build, 0)
        halves = []
        for h in range(2):

            def build_left(b, inner):
                rows = pl.ds(pl.multiple_of(b * BLK, BLK), BLK)
                code = codes[pl.ds(base + h * 8, 8), rows] & (HI - 1)
                for m in range(8):
                    left[m * HI:(m + 1) * HI, rows] = jnp.where(code[m:m + 1, :] == hi_rows, 1.0, 0.0).astype(BF16)
                return inner

            lax.fori_loop(0, BDEV, build_left, 0)
            sums = jnp.dot(left[...], right[h], preferred_element_type=F32)
            picked = jnp.zeros((HI, 2 * LANES), F32)
            for m in range(8):
                picked = picked + jnp.where((lane_r % 64) // 8 == m, sums[m * HI:(m + 1) * HI, :], 0.0)
            halves.append(picked)
        for p in range(2):
            a = halves[0][:, p * LANES:(p + 1) * LANES]
            c = halves[1][:, p * LANES:(p + 1) * LANES]
            totals[(2 * p) * HI:(2 * p + 1) * HI, cols] = jnp.where(lane_c < 64, a, pltpu.roll(c, 64, 1))
            totals[(2 * p + 1) * HI:(2 * p + 2) * HI, cols] = jnp.where(lane_c < 64, pltpu.roll(a, 64, 1), c)
        found = jnp.dot(left_c[...], right_c[...], preferred_element_type=F32)
        picked = jnp.zeros((16, 2 * LANES), F32)
        for m in range(16):
            picked = picked + jnp.where(lane_16 % 16 == m, found[m * 16:(m + 1) * 16, :], 0.0)
        for q in range(16):
            part = picked[:, (q // 8) * LANES:(q // 8 + 1) * LANES]
            moved = pltpu.roll(part, (g * 16 - (q % 8) * 16) % LANES, 1)
            totals[q * 16:(q + 1) * 16, D:] += jnp.where(lane_c[:16] // 16 == g, moved, 0.0)
        return carry

    lax.fori_loop(0, CHUNKS, group, 0)

    slab = KS // N_INGEST
    ring_copies = []
    for o in range(1, N_INGEST):
        target = (i + o) % N_INGEST
        copy = pltpu.make_async_remote_copy(
            src_ref=totals.at[pl.ds(pl.multiple_of(target * slab, slab), slab), :], dst_ref=ring_in.at[o],
            send_sem=s_ring.at[o], recv_sem=r_ring.at[o], device_id=(target, j), device_id_type=MESH)
        copy.start()
        ring_copies.append(copy)

    for d in FAR:
        for e in FAR:
            for r in range(2):
                owner = at(e, 0) if r == 0 else at(0, e)
                origin = at(0, -d) if r == 0 else at(-d, 0)
                first[r, d, e].wait_recv()
                copy = pltpu.make_async_remote_copy(
                    src_ref=mid.at[r, d, e], dst_ref=landed.at[origin * 2 + r], send_sem=s2.at[r, d, e],
                    recv_sem=r2.at[r, d, e], device_id=(i, owner), device_id_type=MESH)
                copy.start()
                second.append(copy)

    for copy in ring_copies:
        copy.wait_recv()
    whole = totals[pl.ds(pl.multiple_of(i * slab, slab), slab), :]
    for o in range(1, N_INGEST):
        whole = whole + ring_in[o]
    ring_sum[...] = whole
    zero_row = jnp.zeros((1, LANES), F32)
    for o in range(N_LIST):
        target = at(o // 4, o % 4)
        eight = ring_sum[pl.ds(pl.multiple_of((target // 4) * 8, 8), 8), :]
        rows = []
        for r in range(2):
            row = jnp.sum(jnp.where(iota((8, WIDE), 0) == (target % 4) * 2 + r, eight, 0.0), axis=0, keepdims=True)
            rows += [row[:, k * LANES:(k + 1) * LANES] for k in range(CHUNKS + 1)] + [zero_row]
        part_out[o] = jnp.concatenate(rows, axis=0)
    part_copies = []
    for o in range(1, N_LIST):
        copy = pltpu.make_async_remote_copy(
            src_ref=part_out.at[o], dst_ref=part_in.at[o], send_sem=s_part.at[o], recv_sem=r_part.at[o],
            device_id=(i, at(o // 4, o % 4)), device_id_type=MESH)
        copy.start()
        part_copies.append(copy)

    def finish(slot, r):
        source = slot // 2
        centre = centre_rows[source].astype(F32)[r * 8:(r + 1) * 8]
        rotated = rotate(landed[slot], centre)
        landed[slot] = jnp.where(ids_smem[source, 0, r] >= 0, rotated, 0.0).astype(BF16)

    def arrival(d, e):
        for r in range(2):
            origin = at(4 - e, 4 - d) if r == 0 else at(4 - d, 4 - e)
            slot = origin * 2 + r
            pltpu.make_async_remote_copy(
                src_ref=stage.at[0], dst_ref=landed.at[slot], send_sem=s2.at[r, d, e], recv_sem=r2.at[r, d, e],
                device_id=(i, origin), device_id_type=MESH).wait_recv()
            finish(slot, r)

    for r in range(2):
        finish(j * 2 + r, r)

    def near_first(t, carry):
        arrival(t + 1, 0)
        return carry

    def near_second(t, carry):
        arrival(0, t + 1)
        return carry

    def far(t, carry):
        arrival((t // 3 * 2) % 3 + 1, (t % 3 * 2) % 3 + 1)
        return carry

    lax.fori_loop(0, 3, near_first, 0)
    lax.fori_loop(0, 3, near_second, 0)
    for copy in part_copies:
        copy.wait_recv()
    total = part_out[0]
    for o in range(1, N_LIST):
        total = total + part_in[o]
    share[...] = total
    lax.fori_loop(0, 9, far, 0)

    for copy in id_copies + row_copies + ring_copies + part_copies + list(first.values()) + second:
        copy.wait_send()


def deliver(landed, share, stored, sums, counts, sem):
    whole = pltpu.make_async_copy(landed, stored, sem.at[0])
    whole.start()
    for r in range(2):
        for k in range(CHUNKS):
            sums[r:r + 1, k * LANES:(k + 1) * LANES] = share[r * 8 + k:r * 8 + k + 1, :]
        counts[r:r + 1, :] = share[r * 8 + CHUNKS:r * 8 + CHUNKS + 1, :M]
    whole.wait()


def shards(vectors, list_ids, code_ids, block_counts, centroids, rotation):
    hbm = pl.BlockSpec(memory_space=pl.ANY)
    smem = pl.BlockSpec(memory_space=pltpu.SMEM)
    vmem = pl.BlockSpec(memory_space=pltpu.VMEM)
    dma = pltpu.SemaphoreType.DMA
    landed, _, share = pl.pallas_call(
        exchange,
        out_shape=(
            pltpu.VMEM((2 * N_LIST, BLK, D), BF16),
            jax.ShapeDtypeStruct((2, 4, 4, BLK, D), BF16),
            pltpu.VMEM((16, LANES), F32),
        ),
        in_specs=[hbm, smem, hbm, smem, hbm, hbm],
        out_specs=(vmem, hbm, vmem),
        scratch_shapes=[
            pltpu.VMEM((BDEV, BLK, D), BF16),
            pltpu.VMEM((M, ROWS_DEV), jnp.int32),
            pltpu.VMEM((LIST_DEV // 16, 16, D), BF16),
            pltpu.VMEM((D, D), BF16),
            pltpu.VMEM((2 * N_LIST - 2, BLK, D), BF16),
            pltpu.VMEM((N_LIST, 8, LANES), jnp.int32),
            pltpu.VMEM((N_LIST, 8, LANES), jnp.int32),
            pltpu.SMEM((N_LIST, 8, LANES), jnp.int32),
            pltpu.VMEM((N_LIST, 16, LANES), BF16),
            pltpu.VMEM((N_LIST, 16, LANES), BF16),
            pltpu.SMEM((BDEV,), jnp.int32),
            pltpu.VMEM((BDEV, BLK, 2 * LANES), BF16),
            pltpu.VMEM((8 * HI, ROWS_DEV), BF16),
            pltpu.VMEM((2, ROWS_DEV, 2 * LANES), BF16),
            pltpu.VMEM((2 * LANES, ROWS_DEV), BF16),
            pltpu.VMEM((ROWS_DEV, 2 * LANES), BF16),
            pltpu.VMEM((KS, WIDE), F32),
            pltpu.VMEM((N_INGEST, KS // N_INGEST, WIDE), F32),
            pltpu.VMEM((KS // N_INGEST, WIDE), F32),
            pltpu.VMEM((N_LIST, 16, LANES), F32),
            pltpu.VMEM((N_LIST, 16, LANES), F32),
            dma((4,)), dma((1,)),
            dma((2, 4, 4)), dma((2, 4, 4)), dma((2, 4, 4)), dma((2, 4, 4)),
            dma((N_LIST,)), dma((N_LIST,)), dma((N_LIST,)), dma((N_LIST,)),
            dma((N_INGEST,)), dma((N_INGEST,)), dma((N_LIST,)), dma((N_LIST,)),
        ],
        compiler_params=pltpu.CompilerParams(
            collective_id=1, has_side_effects=True, vmem_limit_bytes=47 * 1024 * 1024),
        name="exchange",
    )(
        vectors.reshape(BDEV, BLK, D), list_ids, code_ids.T, block_counts,
        centroids.reshape(LIST_DEV // 16, 16, D), rotation,
    )
    stored, sums, counts = pl.pallas_call(
        deliver,
        out_shape=(
            jax.ShapeDtypeStruct((2 * N_LIST, BLK, D), BF16),
            jax.ShapeDtypeStruct((2, D), F32),
            jax.ShapeDtypeStruct((2, M), F32),
        ),
        in_specs=[vmem, vmem],
        out_specs=(hbm, vmem, vmem),
        scratch_shapes=[dma((1,))],
        compiler_params=pltpu.CompilerParams(vmem_limit_bytes=16 * 1024 * 1024),
        name="deliver",
    )(landed, share)
    return stored.reshape(2 * N_LIST * BLK, D), sums, counts


def solution(mesh):
    both = ("ingest", "list")
    in_specs = (P(both, None), P(both), P(both, None), P(both, None), P("list", None), P())
    out_specs = (P(both, None), P(both, None), P(both, None))
    return jax.shard_map(shards, mesh=mesh, in_specs=in_specs, out_specs=out_specs, check_vma=False)
```

```python
import jax
import jax.numpy as jnp
from jax import lax
from jax.experimental import pallas as pl
from jax.experimental.pallas import tpu as pltpu
from jax.sharding import PartitionSpec as P

M = 96
D = 768
KS = 256
LIST_DEV = 4096
BLK = 256
BDEV = 12
ROWS_DEV = BDEV * BLK
N_LIST = 16
N_INGEST = 8
LANES = 128
CHUNKS = D // LANES
WIDE = D + LANES
HI = 64
MESH = pl.DeviceIdType.MESH
F32 = jnp.float32
BF16 = jnp.bfloat16
FAR = (1, 3, 2)


RAW = ((1, 1), (3, 1), (1, 3), (3, 3))
LATER = ((2, 1), (2, 3), (1, 2), (3, 2), (2, 2))
LAST = ((1, 0), (3, 0), (2, 0), (0, 1), (0, 3), (0, 2))


def iota(shape, axis):
    return lax.broadcasted_iota(jnp.int32, shape, axis)


def exchange(
    vec_hbm, lists, codes_hbm, counts, cent_hbm, rot_hbm,
    landed, mid, share,
    vec, codes, cent, rot, stage, ids_out, ids_in, ids_smem, centre_rows, rows_in, table,
    natural, left, right, left_c, right_c, totals, ring_in, ring_sum, part_out, part_in,
    load_sem, smem_sem, s1, r1, s2, r2, s_ids, r_ids, s_rows, r_rows, s_ring, r_ring, s_part, r_part,
):
    i = lax.axis_index("ingest")
    j = lax.axis_index("list")
    y = j // 4
    z = j % 4

    def at(dy, dz):
        return ((y + dy) % 4) * 4 + (z + dz) % 4

    loads = [
        pltpu.make_async_copy(vec_hbm, vec, load_sem.at[0]),
        pltpu.make_async_copy(cent_hbm, cent, load_sem.at[1]),
        pltpu.make_async_copy(codes_hbm, codes, load_sem.at[2]),
        pltpu.make_async_copy(rot_hbm, rot, load_sem.at[3]),
    ]
    loads[0].start()

    barrier = pltpu.get_barrier_semaphore()
    for o in range(1, N_LIST):
        pl.semaphore_signal(barrier, inc=1, device_id=(i, at(o // 4, o % 4)), device_id_type=MESH)
    for o in range(1, N_INGEST):
        pl.semaphore_signal(barrier, inc=1, device_id=((i + o) % N_INGEST, j), device_id_type=MESH)

    owners = [lists[b] >> 12 for b in range(BDEV)]
    slots = []
    for b in range(BDEV):
        rank = jnp.int32(0)
        for c in range(b):
            rank = rank + jnp.where(owners[c] == owners[b], 1, 0)
        limit = jnp.int32(0)
        for o in range(N_LIST):
            limit = jnp.where(owners[b] == o, counts[0, o], limit)
        slots.append(jnp.where(rank < limit, owners[b] * 2 + rank, -1))
    for b in range(BDEV):
        table[b] = slots[b]

    def source_of(slot):
        block = jnp.int32(0)
        for b in range(1, BDEV):
            block = jnp.where(slots[b] == slot, b, block)
        return block

    def list_of(slot):
        found = jnp.int32(-1)
        for b in range(BDEV):
            found = jnp.where(slots[b] == slot, lists[b] & (LIST_DEV - 1), found)
        return found

    lane8 = iota((8, LANES), 1)
    for o in range(N_LIST):
        owner = at(o // 4, o % 4)
        ids_out[o] = jnp.where(lane8 == 0, list_of(owner * 2), list_of(owner * 2 + 1))
    ids_in[j] = ids_out[0]

    pl.semaphore_wait(barrier, N_LIST - 1 + N_INGEST - 1)

    id_copies = []
    for o in range(1, N_LIST):
        copy = pltpu.make_async_remote_copy(
            src_ref=ids_out.at[o], dst_ref=ids_in.at[j], send_sem=s_ids.at[o], recv_sem=r_ids.at[o],
            device_id=(i, at(o // 4, o % 4)), device_id_type=MESH)
        copy.start()
        id_copies.append(copy)

    for load in loads[1:]:
        load.start()
    loads[0].wait()

    hops = {}

    def send(place, d, e, r, packed):
        stage[place] = packed
        along = (0, d) if r == 0 else (d, 0)
        if d == 0:
            along = (e, 0) if r == 0 else (0, e)
        if d == 0 or e == 0:
            landing, gone, come = landed.at[j * 2 + r], s2.at[r, d, e], r2.at[r, d, e]
        else:
            landing, gone, come = mid.at[r, d, e], s1.at[r, d, e], r1.at[r, d, e]
        copy = pltpu.make_async_remote_copy(
            src_ref=stage.at[place], dst_ref=landing, send_sem=gone, recv_sem=come,
            device_id=(i, at(*along)), device_id_type=MESH)
        copy.start()
        hops[r, d, e] = copy

    def slot_of(d, e, r):
        return (at(e, d) if r == 0 else at(d, e)) * 2 + r

    def send_raw(first, pairs):
        for n, (d, e) in enumerate(pairs):
            for r in range(2):
                send(first + 2 * n + r, d, e, r, vec[source_of(slot_of(d, e, r))])

    send_raw(0, RAW[:2])

    for copy in id_copies:
        copy.wait_recv()
    to_smem = pltpu.make_async_copy(ids_in, ids_smem, smem_sem.at[0])
    to_smem.start()
    to_smem.wait()
    loads[1].wait()
    sub16 = iota((16, D), 0)
    pad = jnp.zeros((2, LANES), F32)
    row_copies = []
    for o in range(N_LIST):
        source = at(-(o // 4) % 4, -(o % 4) % 4)
        parts = []
        for r in range(2):
            wanted = jnp.maximum(ids_smem[source, 0, r], 0)
            near = cent[wanted >> 4].astype(F32)
            row = jnp.sum(jnp.where(sub16 == (wanted & 15), near, 0.0), axis=0, keepdims=True)
            parts += [row[:, k * LANES:(k + 1) * LANES] for k in range(CHUNKS)] + [pad]
        centre_rows[source] = jnp.concatenate(parts, axis=0).astype(BF16)
        if o == 0:
            rows_in[j] = centre_rows[source]
        else:
            copy = pltpu.make_async_remote_copy(
                src_ref=centre_rows.at[source], dst_ref=rows_in.at[j], send_sem=s_rows.at[o], recv_sem=r_rows.at[o],
                device_id=(i, source), device_id_type=MESH)
            copy.start()
            row_copies.append(copy)

    send_raw(4, RAW[2:])
    loads[2].wait()
    loads[3].wait()
    for copy in row_copies:
        copy.wait_recv()

    eye = (iota((BLK, BLK), 0) == iota((BLK, BLK), 1)).astype(BF16)
    none = jnp.zeros((LANES - M, BLK), F32)

    def rotate(rows, centre):
        residual = jnp.concatenate([
            (rows[:, k * LANES:(k + 1) * LANES].astype(F32) - centre[k:k + 1, :]).astype(BF16) for k in range(CHUNKS)
        ], axis=1)
        return jnp.dot(residual, rot[...], preferred_element_type=F32)

    def encode(b, carry):
        slot = table[b]
        kept = slot >= 0
        slot = jnp.maximum(slot, 0)
        tile = rows_in[slot >> 1].astype(F32)
        centre = jnp.where((slot & 1) == 0, tile[0:8], tile[8:16])
        vec[b] = jnp.where(kept, rotate(vec[b], centre), 0.0).astype(BF16)
        code = codes[:, pl.ds(pl.multiple_of(b * BLK, BLK), BLK)]
        both = jnp.concatenate([
            (code >> 6).astype(F32), none, jnp.where(kept, (code >> 4).astype(F32), -1.0), none], axis=0).astype(BF16)
        natural[b] = lax.dot_general(
            eye, both, (((1,), (1,)), ((), ())), preferred_element_type=F32).astype(BF16)
        return carry

    lax.fori_loop(0, BDEV, encode, 0)

    def encoded(slot):
        filled = jnp.int32(0)
        for b in range(BDEV):
            filled = filled + jnp.where(slots[b] == slot, 1, 0)
        return jnp.where(filled > 0, vec[source_of(slot)], jnp.zeros((BLK, D), BF16))

    place = 8
    for d, e in LATER + LAST:
        for r in range(2):
            send(place, d, e, r, encoded(slot_of(d, e, r)))
            place += 1
    for r in range(2):
        landed[j * 2 + r] = encoded(j * 2 + r)

    totals[:, D:] = jnp.zeros((KS, LANES), F32)
    lane = iota((BLK, LANES), 1)
    upper = (lane >= 64).astype(F32)
    lane_r = iota((HI, 2 * LANES), 1)
    lane_c = iota((HI, LANES), 1)
    lane_16 = iota((16, 2 * LANES), 1)
    hi_rows = iota((HI, BLK), 0)
    wide_row = iota((LANES, 2 * LANES), 0)
    wide_lane = iota((LANES, 2 * LANES), 1)
    digit = (iota((BLK, 2 * LANES), 1) // 16).astype(F32)

    second = {}
    for d, e in RAW + LATER:
        for r in range(2):
            owner = at(e, 0) if r == 0 else at(0, e)
            origin = at(0, -d) if r == 0 else at(-d, 0)
            second[r, d, e] = pltpu.make_async_remote_copy(
                src_ref=mid.at[r, d, e], dst_ref=landed.at[origin * 2 + r], send_sem=s2.at[r, d, e],
                recv_sem=r2.at[r, d, e], device_id=(i, owner), device_id_type=MESH)

    def forward(pairs):
        for d, e in pairs:
            for r in range(2):
                hops[r, d, e].wait_recv()
                second[r, d, e].start()

    def group(g, carry):
        @pl.when(g == 1)
        def early():
            forward(RAW[:2])

        @pl.when(g == 3)
        def next():
            forward(RAW[2:])

        spread = (wide_row == g * 16 + (wide_lane // LANES) * 8 + (wide_lane % 64) // 8).astype(BF16)
        spread_c = (wide_row == g * 16 + wide_lane % 16).astype(BF16)
        cols = pl.ds(pl.multiple_of(g * LANES, LANES), LANES)
        base = pl.multiple_of(g * 16, 16)

        def build(b, inner):
            rows = pl.ds(pl.multiple_of(b * BLK, BLK), BLK)
            lo = jnp.dot(natural[b, :, :LANES], spread, preferred_element_type=F32)
            e = vec[b, :, cols].astype(F32)
            turned = pltpu.roll(e, 64, 1)
            for h in range(2):
                both = jnp.where(lane < 64, e, turned) if h == 0 else jnp.where(lane < 64, turned, e)
                lo_h = lo[:, h * LANES:(h + 1) * LANES]
                for p in range(2):
                    right[h, rows, p * LANES:(p + 1) * LANES] = jnp.where(
                        lo_h == upper + float(2 * p), both, 0.0).astype(BF16)
            high = jnp.dot(natural[b, :, LANES:], spread_c, preferred_element_type=F32)
            right_c[rows, :] = jnp.where(high == digit, 1.0, 0.0).astype(BF16)
            code = codes[pl.ds(base, 16), rows] & 15
            for m in range(16):
                left_c[m * 16:(m + 1) * 16, rows] = jnp.where(
                    code[m:m + 1, :] == hi_rows[:16], 1.0, 0.0).astype(BF16)
            return inner

        lax.fori_loop(0, BDEV, build, 0)
        halves = []
        for h in range(2):

            def build_left(b, inner):
                rows = pl.ds(pl.multiple_of(b * BLK, BLK), BLK)
                code = codes[pl.ds(base + h * 8, 8), rows] & (HI - 1)
                for m in range(8):
                    left[m * HI:(m + 1) * HI, rows] = jnp.where(code[m:m + 1, :] == hi_rows, 1.0, 0.0).astype(BF16)
                return inner

            lax.fori_loop(0, BDEV, build_left, 0)
            sums = jnp.dot(left[...], right[h], preferred_element_type=F32)
            picked = jnp.zeros((HI, 2 * LANES), F32)
            for m in range(8):
                picked = picked + jnp.where((lane_r % 64) // 8 == m, sums[m * HI:(m + 1) * HI, :], 0.0)
            halves.append(picked)
        for p in range(2):
            a = halves[0][:, p * LANES:(p + 1) * LANES]
            c = halves[1][:, p * LANES:(p + 1) * LANES]
            totals[(2 * p) * HI:(2 * p + 1) * HI, cols] = jnp.where(lane_c < 64, a, pltpu.roll(c, 64, 1))
            totals[(2 * p + 1) * HI:(2 * p + 2) * HI, cols] = jnp.where(lane_c < 64, pltpu.roll(a, 64, 1), c)
        found = jnp.dot(left_c[...], right_c[...], preferred_element_type=F32)
        picked = jnp.zeros((16, 2 * LANES), F32)
        for m in range(16):
            picked = picked + jnp.where(lane_16 % 16 == m, found[m * 16:(m + 1) * 16, :], 0.0)
        for q in range(16):
            part = picked[:, (q // 8) * LANES:(q // 8 + 1) * LANES]
            moved = pltpu.roll(part, (g * 16 - (q % 8) * 16) % LANES, 1)
            totals[q * 16:(q + 1) * 16, D:] += jnp.where(lane_c[:16] // 16 == g, moved, 0.0)
        return carry

    lax.fori_loop(0, CHUNKS, group, 0)

    slab = KS // N_INGEST
    ring_copies = []
    for o in range(1, N_INGEST):
        target = (i + o) % N_INGEST
        copy = pltpu.make_async_remote_copy(
            src_ref=totals.at[pl.ds(pl.multiple_of(target * slab, slab), slab), :], dst_ref=ring_in.at[o],
            send_sem=s_ring.at[o], recv_sem=r_ring.at[o], device_id=(target, j), device_id_type=MESH)
        copy.start()
        ring_copies.append(copy)

    forward(LATER)

    for copy in ring_copies:
        copy.wait_recv()
    whole = totals[pl.ds(pl.multiple_of(i * slab, slab), slab), :]
    for o in range(1, N_INGEST):
        whole = whole + ring_in[o]
    ring_sum[...] = whole
    zero_row = jnp.zeros((1, LANES), F32)
    for o in range(N_LIST):
        target = at(o // 4, o % 4)
        eight = ring_sum[pl.ds(pl.multiple_of((target // 4) * 8, 8), 8), :]
        rows = []
        for r in range(2):
            row = jnp.sum(jnp.where(iota((8, WIDE), 0) == (target % 4) * 2 + r, eight, 0.0), axis=0, keepdims=True)
            rows += [row[:, k * LANES:(k + 1) * LANES] for k in range(CHUNKS + 1)] + [zero_row]
        part_out[o] = jnp.concatenate(rows, axis=0)
    part_copies = []
    for o in range(1, N_LIST):
        copy = pltpu.make_async_remote_copy(
            src_ref=part_out.at[o], dst_ref=part_in.at[o], send_sem=s_part.at[o], recv_sem=r_part.at[o],
            device_id=(i, at(o // 4, o % 4)), device_id_type=MESH)
        copy.start()
        part_copies.append(copy)

    def finish(slot, r):
        source = slot // 2
        centre = centre_rows[source].astype(F32)[r * 8:(r + 1) * 8]
        rotated = rotate(landed[slot], centre)
        landed[slot] = jnp.where(ids_smem[source, 0, r] >= 0, rotated, 0.0).astype(BF16)

    def arrival(t, carry):
        d, e = 1 + 2 * (t % 2), 1 + 2 * (t // 2)
        for r in range(2):
            origin = at(4 - e, 4 - d) if r == 0 else at(4 - d, 4 - e)
            slot = origin * 2 + r
            pltpu.make_async_remote_copy(
                src_ref=stage.at[0], dst_ref=landed.at[slot], send_sem=s2.at[r, d, e], recv_sem=r2.at[r, d, e],
                device_id=(i, origin), device_id_type=MESH).wait_recv()
            finish(slot, r)
        return carry

    lax.fori_loop(0, 4, arrival, 0)

    for copy in part_copies:
        copy.wait_recv()
    total = part_out[0]
    for o in range(1, N_LIST):
        total = total + part_in[o]
    share[...] = total

    for d, e in LATER + LAST:
        for r in range(2):
            (hops[r, d, e] if d == 0 or e == 0 else second[r, d, e]).wait_recv()
    for copy in id_copies + row_copies + ring_copies + part_copies + list(hops.values()) + list(second.values()):
        copy.wait_send()


def deliver(landed, share, stored, sums, counts, sem):
    parts = [
        pltpu.make_async_copy(landed.at[pl.ds(n * 4, 4)], stored.at[pl.ds(n * 4, 4)], sem.at[n]) for n in range(8)
    ]
    for part in parts:
        part.start()
    for r in range(2):
        for k in range(CHUNKS):
            sums[r:r + 1, k * LANES:(k + 1) * LANES] = share[r * 8 + k:r * 8 + k + 1, :]
        counts[r:r + 1, :] = share[r * 8 + CHUNKS:r * 8 + CHUNKS + 1, :M]
    for part in parts:
        part.wait()


def shards(vectors, list_ids, code_ids, block_counts, centroids, rotation):
    hbm = pl.BlockSpec(memory_space=pl.ANY)
    smem = pl.BlockSpec(memory_space=pltpu.SMEM)
    vmem = pl.BlockSpec(memory_space=pltpu.VMEM)
    dma = pltpu.SemaphoreType.DMA
    landed, _, share = pl.pallas_call(
        exchange,
        out_shape=(
            pltpu.VMEM((2 * N_LIST, BLK, D), BF16),
            jax.ShapeDtypeStruct((2, 4, 4, BLK, D), BF16),
            pltpu.VMEM((16, LANES), F32),
        ),
        in_specs=[hbm, smem, hbm, smem, hbm, hbm],
        out_specs=(vmem, hbm, vmem),
        scratch_shapes=[
            pltpu.VMEM((BDEV, BLK, D), BF16),
            pltpu.VMEM((M, ROWS_DEV), jnp.int32),
            pltpu.VMEM((LIST_DEV // 16, 16, D), BF16),
            pltpu.VMEM((D, D), BF16),
            pltpu.VMEM((2 * N_LIST - 2, BLK, D), BF16),
            pltpu.VMEM((N_LIST, 8, LANES), jnp.int32),
            pltpu.VMEM((N_LIST, 8, LANES), jnp.int32),
            pltpu.SMEM((N_LIST, 8, LANES), jnp.int32),
            pltpu.VMEM((N_LIST, 16, LANES), BF16),
            pltpu.VMEM((N_LIST, 16, LANES), BF16),
            pltpu.SMEM((BDEV,), jnp.int32),
            pltpu.VMEM((BDEV, BLK, 2 * LANES), BF16),
            pltpu.VMEM((8 * HI, ROWS_DEV), BF16),
            pltpu.VMEM((2, ROWS_DEV, 2 * LANES), BF16),
            pltpu.VMEM((2 * LANES, ROWS_DEV), BF16),
            pltpu.VMEM((ROWS_DEV, 2 * LANES), BF16),
            pltpu.VMEM((KS, WIDE), F32),
            pltpu.VMEM((N_INGEST, KS // N_INGEST, WIDE), F32),
            pltpu.VMEM((KS // N_INGEST, WIDE), F32),
            pltpu.VMEM((N_LIST, 16, LANES), F32),
            pltpu.VMEM((N_LIST, 16, LANES), F32),
            dma((4,)), dma((1,)),
            dma((2, 4, 4)), dma((2, 4, 4)), dma((2, 4, 4)), dma((2, 4, 4)),
            dma((N_LIST,)), dma((N_LIST,)), dma((N_LIST,)), dma((N_LIST,)),
            dma((N_INGEST,)), dma((N_INGEST,)), dma((N_LIST,)), dma((N_LIST,)),
        ],
        compiler_params=pltpu.CompilerParams(
            collective_id=1, has_side_effects=True, vmem_limit_bytes=47 * 1024 * 1024),
        name="exchange",
    )(
        vectors.reshape(BDEV, BLK, D), list_ids, code_ids.T, block_counts,
        centroids.reshape(LIST_DEV // 16, 16, D), rotation,
    )
    stored, sums, counts = pl.pallas_call(
        deliver,
        out_shape=(
            jax.ShapeDtypeStruct((2 * N_LIST, BLK, D), BF16),
            jax.ShapeDtypeStruct((2, D), F32),
            jax.ShapeDtypeStruct((2, M), F32),
        ),
        in_specs=[vmem, vmem],
        out_specs=(hbm, vmem, vmem),
        scratch_shapes=[dma((8,))],
        compiler_params=pltpu.CompilerParams(vmem_limit_bytes=16 * 1024 * 1024),
        name="deliver",
    )(landed, share)
    return stored.reshape(2 * N_LIST * BLK, D), sums, counts


def solution(mesh):
    both = ("ingest", "list")
    in_specs = (P(both, None), P(both), P(both, None), P(both, None), P("list", None), P())
    out_specs = (P(both, None), P(both, None), P(both, None))
    return jax.shard_map(shards, mesh=mesh, in_specs=in_specs, out_specs=out_specs, check_vma=False)
```

```python
import jax
import jax.numpy as jnp
from jax import lax
from jax.experimental import pallas as pl
from jax.experimental.pallas import tpu as pltpu
from jax.sharding import PartitionSpec as P

M = 96
D = 768
KS = 256
LIST_DEV = 4096
BLK = 256
BDEV = 12
ROWS_DEV = BDEV * BLK
N_LIST = 16
N_INGEST = 8
LANES = 128
CHUNKS = D // LANES
WIDE = D + LANES
HI = 64
MESH = pl.DeviceIdType.MESH
F32 = jnp.float32
BF16 = jnp.bfloat16
FAR = (1, 3, 2)


RAW = ((1, 1), (3, 1), (1, 3), (3, 3))
LATER = ((2, 1), (2, 3), (1, 2), (3, 2), (2, 2))
LAST = ((1, 0), (3, 0), (2, 0), (0, 1), (0, 3), (0, 2))


def iota(shape, axis):
    return lax.broadcasted_iota(jnp.int32, shape, axis)


def exchange(
    vec_hbm, lists, codes_hbm, counts, cent_hbm, rot_hbm,
    landed, mid, share,
    vec, codes, cent, rot, stage, ids_out, ids_in, ids_smem, centre_rows, rows_in, table,
    natural, left, right, left_c, right_c, totals, ring_in, ring_sum, part_out, part_in,
    load_sem, smem_sem, s1, r1, s2, r2, s_ids, r_ids, s_rows, r_rows, s_ring, r_ring, s_part, r_part,
):
    i = lax.axis_index("ingest")
    j = lax.axis_index("list")
    y = j // 4
    z = j % 4

    def at(dy, dz):
        return ((y + dy) % 4) * 4 + (z + dz) % 4

    loads = [
        pltpu.make_async_copy(vec_hbm, vec, load_sem.at[0]),
        pltpu.make_async_copy(cent_hbm, cent, load_sem.at[1]),
        pltpu.make_async_copy(codes_hbm, codes, load_sem.at[2]),
        pltpu.make_async_copy(rot_hbm, rot, load_sem.at[3]),
    ]
    loads[0].start()

    barrier = pltpu.get_barrier_semaphore()
    for o in range(1, N_LIST):
        pl.semaphore_signal(barrier, inc=1, device_id=(i, at(o // 4, o % 4)), device_id_type=MESH)
    for o in range(1, N_INGEST):
        pl.semaphore_signal(barrier, inc=1, device_id=((i + o) % N_INGEST, j), device_id_type=MESH)

    owners = [lists[b] >> 12 for b in range(BDEV)]
    slots = []
    for b in range(BDEV):
        rank = jnp.int32(0)
        for c in range(b):
            rank = rank + jnp.where(owners[c] == owners[b], 1, 0)
        limit = jnp.int32(0)
        for o in range(N_LIST):
            limit = jnp.where(owners[b] == o, counts[0, o], limit)
        slots.append(jnp.where(rank < limit, owners[b] * 2 + rank, -1))
    for b in range(BDEV):
        table[b] = slots[b]

    def source_of(slot):
        block = jnp.int32(0)
        for b in range(1, BDEV):
            block = jnp.where(slots[b] == slot, b, block)
        return block

    def list_of(slot):
        found = jnp.int32(-1)
        for b in range(BDEV):
            found = jnp.where(slots[b] == slot, lists[b] & (LIST_DEV - 1), found)
        return found

    lane8 = iota((8, LANES), 1)
    for o in range(N_LIST):
        owner = at(o // 4, o % 4)
        ids_out[o] = jnp.where(lane8 == 0, list_of(owner * 2), list_of(owner * 2 + 1))
    ids_in[j] = ids_out[0]

    pl.semaphore_wait(barrier, N_LIST - 1 + N_INGEST - 1)

    id_copies = []
    for o in range(1, N_LIST):
        copy = pltpu.make_async_remote_copy(
            src_ref=ids_out.at[o, pl.ds(0, 1)], dst_ref=ids_in.at[j, pl.ds(0, 1)], send_sem=s_ids.at[o], recv_sem=r_ids.at[o],
            device_id=(i, at(o // 4, o % 4)), device_id_type=MESH)
        copy.start()
        id_copies.append(copy)

    for load in loads[1:]:
        load.start()
    loads[0].wait()

    hops = {}

    def send(place, d, e, r, packed):
        stage[place] = packed
        along = (0, d) if r == 0 else (d, 0)
        if d == 0:
            along = (e, 0) if r == 0 else (0, e)
        if d == 0 or e == 0:
            landing, gone, come = landed.at[j * 2 + r], s2.at[r, d, e], r2.at[r, d, e]
        else:
            landing, gone, come = mid.at[r, d, e], s1.at[r, d, e], r1.at[r, d, e]
        copy = pltpu.make_async_remote_copy(
            src_ref=stage.at[place], dst_ref=landing, send_sem=gone, recv_sem=come,
            device_id=(i, at(*along)), device_id_type=MESH)
        copy.start()
        hops[r, d, e] = copy

    def slot_of(d, e, r):
        return (at(e, d) if r == 0 else at(d, e)) * 2 + r

    def send_raw(first, pairs):
        for n, (d, e) in enumerate(pairs):
            for r in range(2):
                send(first + 2 * n + r, d, e, r, vec[source_of(slot_of(d, e, r))])

    send_raw(0, RAW[:2])

    for copy in id_copies:
        copy.wait_recv()
    to_smem = pltpu.make_async_copy(ids_in, ids_smem, smem_sem.at[0])
    to_smem.start()
    to_smem.wait()
    loads[1].wait()
    sub16 = iota((16, D), 0)
    pad = jnp.zeros((2, LANES), F32)
    row_copies = []
    for o in range(N_LIST):
        source = at(-(o // 4) % 4, -(o % 4) % 4)
        parts = []
        for r in range(2):
            wanted = jnp.maximum(ids_smem[source, 0, r], 0)
            near = cent[wanted >> 4].astype(F32)
            row = jnp.sum(jnp.where(sub16 == (wanted & 15), near, 0.0), axis=0, keepdims=True)
            parts += [row[:, k * LANES:(k + 1) * LANES] for k in range(CHUNKS)] + [pad]
        centre_rows[source] = jnp.concatenate(parts, axis=0).astype(BF16)
        if o == 0:
            rows_in[j] = centre_rows[source]
        else:
            copy = pltpu.make_async_remote_copy(
                src_ref=centre_rows.at[source], dst_ref=rows_in.at[j], send_sem=s_rows.at[o], recv_sem=r_rows.at[o],
                device_id=(i, source), device_id_type=MESH)
            copy.start()
            row_copies.append(copy)

    send_raw(4, RAW[2:])
    loads[2].wait()
    loads[3].wait()
    for copy in row_copies:
        copy.wait_recv()

    eye = (iota((BLK, BLK), 0) == iota((BLK, BLK), 1)).astype(BF16)
    none = jnp.zeros((LANES - M, BLK), F32)

    def rotate(rows, centre):
        residual = jnp.concatenate([
            (rows[:, k * LANES:(k + 1) * LANES].astype(F32) - centre[k:k + 1, :]).astype(BF16) for k in range(CHUNKS)
        ], axis=1)
        return jnp.dot(residual, rot[...], preferred_element_type=F32)

    def encode(b, carry):
        slot = table[b]
        kept = slot >= 0
        slot = jnp.maximum(slot, 0)
        tile = rows_in[slot >> 1].astype(F32)
        centre = jnp.where((slot & 1) == 0, tile[0:8], tile[8:16])
        vec[b] = jnp.where(kept, rotate(vec[b], centre), 0.0).astype(BF16)
        code = codes[:, pl.ds(pl.multiple_of(b * BLK, BLK), BLK)]
        both = jnp.concatenate([
            (code >> 6).astype(F32), none, jnp.where(kept, (code >> 4).astype(F32), -1.0), none], axis=0).astype(BF16)
        natural[b] = lax.dot_general(
            eye, both, (((1,), (1,)), ((), ())), preferred_element_type=F32).astype(BF16)
        return carry

    lax.fori_loop(0, BDEV, encode, 0)

    def encoded(slot):
        filled = jnp.int32(0)
        for b in range(BDEV):
            filled = filled + jnp.where(slots[b] == slot, 1, 0)
        return jnp.where(filled > 0, vec[source_of(slot)], jnp.zeros((BLK, D), BF16))

    place = 8
    def send_encoded(first, pairs):
        for n, (d, e) in enumerate(pairs):
            for r in range(2):
                send(first + 2 * n + r, d, e, r, encoded(slot_of(d, e, r)))

    send_encoded(8, LATER)
    for r in range(2):
        landed[j * 2 + r] = encoded(j * 2 + r)

    totals[:, D:] = jnp.zeros((KS, LANES), F32)
    lane = iota((BLK, LANES), 1)
    upper = (lane >= 64).astype(F32)
    lane_r = iota((HI, 2 * LANES), 1)
    lane_c = iota((HI, LANES), 1)
    lane_16 = iota((16, 2 * LANES), 1)
    hi_rows = iota((HI, BLK), 0)
    wide_row = iota((LANES, 2 * LANES), 0)
    wide_lane = iota((LANES, 2 * LANES), 1)
    digit = (iota((BLK, 2 * LANES), 1) // 16).astype(F32)

    second = {}
    for d, e in RAW + LATER:
        for r in range(2):
            owner = at(e, 0) if r == 0 else at(0, e)
            origin = at(0, -d) if r == 0 else at(-d, 0)
            second[r, d, e] = pltpu.make_async_remote_copy(
                src_ref=mid.at[r, d, e], dst_ref=landed.at[origin * 2 + r], send_sem=s2.at[r, d, e],
                recv_sem=r2.at[r, d, e], device_id=(i, owner), device_id_type=MESH)

    def forward(pairs):
        for d, e in pairs:
            for r in range(2):
                hops[r, d, e].wait_recv()
                second[r, d, e].start()

    def group(g, carry):
        @pl.when(g == 1)
        def early():
            forward(RAW[:2])

        @pl.when(g == 3)
        def next():
            forward(RAW[2:])

        spread = (wide_row == g * 16 + (wide_lane // LANES) * 8 + (wide_lane % 64) // 8).astype(BF16)
        spread_c = (wide_row == g * 16 + wide_lane % 16).astype(BF16)
        cols = pl.ds(pl.multiple_of(g * LANES, LANES), LANES)
        base = pl.multiple_of(g * 16, 16)

        def build(b, inner):
            rows = pl.ds(pl.multiple_of(b * BLK, BLK), BLK)
            lo = jnp.dot(natural[b, :, :LANES], spread, preferred_element_type=F32)
            e = vec[b, :, cols].astype(F32)
            turned = pltpu.roll(e, 64, 1)
            for h in range(2):
                both = jnp.where(lane < 64, e, turned) if h == 0 else jnp.where(lane < 64, turned, e)
                lo_h = lo[:, h * LANES:(h + 1) * LANES]
                for p in range(2):
                    right[h, rows, p * LANES:(p + 1) * LANES] = jnp.where(
                        lo_h == upper + float(2 * p), both, 0.0).astype(BF16)
            high = jnp.dot(natural[b, :, LANES:], spread_c, preferred_element_type=F32)
            right_c[rows, :] = jnp.where(high == digit, 1.0, 0.0).astype(BF16)
            code = codes[pl.ds(base, 16), rows] & 15
            for m in range(16):
                left_c[m * 16:(m + 1) * 16, rows] = jnp.where(
                    code[m:m + 1, :] == hi_rows[:16], 1.0, 0.0).astype(BF16)
            return inner

        lax.fori_loop(0, BDEV, build, 0)
        halves = []
        for h in range(2):

            def build_left(b, inner):
                rows = pl.ds(pl.multiple_of(b * BLK, BLK), BLK)
                code = codes[pl.ds(base + h * 8, 8), rows] & (HI - 1)
                for m in range(8):
                    left[m * HI:(m + 1) * HI, rows] = jnp.where(code[m:m + 1, :] == hi_rows, 1.0, 0.0).astype(BF16)
                return inner

            lax.fori_loop(0, BDEV, build_left, 0)
            sums = jnp.dot(left[...], right[h], preferred_element_type=F32)
            picked = jnp.zeros((HI, 2 * LANES), F32)
            for m in range(8):
                picked = picked + jnp.where((lane_r % 64) // 8 == m, sums[m * HI:(m + 1) * HI, :], 0.0)
            halves.append(picked)
        for p in range(2):
            a = halves[0][:, p * LANES:(p + 1) * LANES]
            c = halves[1][:, p * LANES:(p + 1) * LANES]
            totals[(2 * p) * HI:(2 * p + 1) * HI, cols] = jnp.where(lane_c < 64, a, pltpu.roll(c, 64, 1))
            totals[(2 * p + 1) * HI:(2 * p + 2) * HI, cols] = jnp.where(lane_c < 64, pltpu.roll(a, 64, 1), c)
        found = jnp.dot(left_c[...], right_c[...], preferred_element_type=F32)
        picked = jnp.zeros((16, 2 * LANES), F32)
        for m in range(16):
            picked = picked + jnp.where(lane_16 % 16 == m, found[m * 16:(m + 1) * 16, :], 0.0)
        for q in range(16):
            part = picked[:, (q // 8) * LANES:(q // 8 + 1) * LANES]
            moved = pltpu.roll(part, (g * 16 - (q % 8) * 16) % LANES, 1)
            totals[q * 16:(q + 1) * 16, D:] += jnp.where(lane_c[:16] // 16 == g, moved, 0.0)
        return carry

    lax.fori_loop(0, CHUNKS, group, 0)

    slab = KS // N_INGEST
    ring_copies = []
    for o in range(1, N_INGEST):
        target = (i + o) % N_INGEST
        copy = pltpu.make_async_remote_copy(
            src_ref=totals.at[pl.ds(pl.multiple_of(target * slab, slab), slab), :], dst_ref=ring_in.at[o],
            send_sem=s_ring.at[o], recv_sem=r_ring.at[o], device_id=(target, j), device_id_type=MESH)
        copy.start()
        ring_copies.append(copy)

    send_encoded(18, LAST)

    for copy in ring_copies:
        copy.wait_recv()
    whole = totals[pl.ds(pl.multiple_of(i * slab, slab), slab), :]
    for o in range(1, N_INGEST):
        whole = whole + ring_in[o]
    ring_sum[...] = whole
    zero_row = jnp.zeros((1, LANES), F32)
    for o in range(N_LIST):
        target = at(o // 4, o % 4)
        eight = ring_sum[pl.ds(pl.multiple_of((target // 4) * 8, 8), 8), :]
        rows = []
        for r in range(2):
            row = jnp.sum(jnp.where(iota((8, WIDE), 0) == (target % 4) * 2 + r, eight, 0.0), axis=0, keepdims=True)
            rows += [row[:, k * LANES:(k + 1) * LANES] for k in range(CHUNKS + 1)] + [zero_row]
        part_out[o] = jnp.concatenate(rows, axis=0)
    part_copies = []
    for o in range(1, N_LIST):
        copy = pltpu.make_async_remote_copy(
            src_ref=part_out.at[o], dst_ref=part_in.at[o], send_sem=s_part.at[o], recv_sem=r_part.at[o],
            device_id=(i, at(o // 4, o % 4)), device_id_type=MESH)
        copy.start()
        part_copies.append(copy)

    forward(LATER)

    def finish(slot, r):
        source = slot // 2
        centre = centre_rows[source].astype(F32)[r * 8:(r + 1) * 8]
        rotated = rotate(landed[slot], centre)
        landed[slot] = jnp.where(ids_smem[source, 0, r] >= 0, rotated, 0.0).astype(BF16)

    def arrival(t, carry):
        d, e = 1 + 2 * (t % 2), 1 + 2 * (t // 2)
        for r in range(2):
            origin = at(4 - e, 4 - d) if r == 0 else at(4 - d, 4 - e)
            slot = origin * 2 + r
            pltpu.make_async_remote_copy(
                src_ref=stage.at[0], dst_ref=landed.at[slot], send_sem=s2.at[r, d, e], recv_sem=r2.at[r, d, e],
                device_id=(i, origin), device_id_type=MESH).wait_recv()
            finish(slot, r)
        return carry

    lax.fori_loop(0, 4, arrival, 0)

    for copy in part_copies:
        copy.wait_recv()
    total = part_out[0]
    for o in range(1, N_LIST):
        total = total + part_in[o]
    share[...] = total

    for d, e in LATER + LAST:
        for r in range(2):
            (hops[r, d, e] if d == 0 or e == 0 else second[r, d, e]).wait_recv()
    for copy in id_copies + row_copies + ring_copies + part_copies + list(hops.values()) + list(second.values()):
        copy.wait_send()


def deliver(landed, share, stored, sums, counts, sem):
    parts = [
        pltpu.make_async_copy(landed.at[pl.ds(n * 4, 4)], stored.at[pl.ds(n * 4, 4)], sem.at[n]) for n in range(8)
    ]
    for part in parts:
        part.start()
    for r in range(2):
        for k in range(CHUNKS):
            sums[r:r + 1, k * LANES:(k + 1) * LANES] = share[r * 8 + k:r * 8 + k + 1, :]
        counts[r:r + 1, :] = share[r * 8 + CHUNKS:r * 8 + CHUNKS + 1, :M]
    for part in parts:
        part.wait()


def shards(vectors, list_ids, code_ids, block_counts, centroids, rotation):
    hbm = pl.BlockSpec(memory_space=pl.ANY)
    smem = pl.BlockSpec(memory_space=pltpu.SMEM)
    vmem = pl.BlockSpec(memory_space=pltpu.VMEM)
    dma = pltpu.SemaphoreType.DMA
    landed, _, share = pl.pallas_call(
        exchange,
        out_shape=(
            pltpu.VMEM((2 * N_LIST, BLK, D), BF16),
            jax.ShapeDtypeStruct((2, 4, 4, BLK, D), BF16),
            pltpu.VMEM((16, LANES), F32),
        ),
        in_specs=[hbm, smem, hbm, smem, hbm, hbm],
        out_specs=(vmem, hbm, vmem),
        scratch_shapes=[
            pltpu.VMEM((BDEV, BLK, D), BF16),
            pltpu.VMEM((M, ROWS_DEV), jnp.int32),
            pltpu.VMEM((LIST_DEV // 16, 16, D), BF16),
            pltpu.VMEM((D, D), BF16),
            pltpu.VMEM((2 * N_LIST - 2, BLK, D), BF16),
            pltpu.VMEM((N_LIST, 8, LANES), jnp.int32),
            pltpu.VMEM((N_LIST, 8, LANES), jnp.int32),
            pltpu.SMEM((N_LIST, 8, LANES), jnp.int32),
            pltpu.VMEM((N_LIST, 16, LANES), BF16),
            pltpu.VMEM((N_LIST, 16, LANES), BF16),
            pltpu.SMEM((BDEV,), jnp.int32),
            pltpu.VMEM((BDEV, BLK, 2 * LANES), BF16),
            pltpu.VMEM((8 * HI, ROWS_DEV), BF16),
            pltpu.VMEM((2, ROWS_DEV, 2 * LANES), BF16),
            pltpu.VMEM((2 * LANES, ROWS_DEV), BF16),
            pltpu.VMEM((ROWS_DEV, 2 * LANES), BF16),
            pltpu.VMEM((KS, WIDE), F32),
            pltpu.VMEM((N_INGEST, KS // N_INGEST, WIDE), F32),
            pltpu.VMEM((KS // N_INGEST, WIDE), F32),
            pltpu.VMEM((N_LIST, 16, LANES), F32),
            pltpu.VMEM((N_LIST, 16, LANES), F32),
            dma((4,)), dma((1,)),
            dma((2, 4, 4)), dma((2, 4, 4)), dma((2, 4, 4)), dma((2, 4, 4)),
            dma((N_LIST,)), dma((N_LIST,)), dma((N_LIST,)), dma((N_LIST,)),
            dma((N_INGEST,)), dma((N_INGEST,)), dma((N_LIST,)), dma((N_LIST,)),
        ],
        compiler_params=pltpu.CompilerParams(
            collective_id=1, has_side_effects=True, vmem_limit_bytes=47 * 1024 * 1024),
        name="exchange",
    )(
        vectors.reshape(BDEV, BLK, D), list_ids, code_ids.T, block_counts,
        centroids.reshape(LIST_DEV // 16, 16, D), rotation,
    )
    stored, sums, counts = pl.pallas_call(
        deliver,
        out_shape=(
            jax.ShapeDtypeStruct((2 * N_LIST, BLK, D), BF16),
            jax.ShapeDtypeStruct((2, D), F32),
            jax.ShapeDtypeStruct((2, M), F32),
        ),
        in_specs=[vmem, vmem],
        out_specs=(hbm, vmem, vmem),
        scratch_shapes=[dma((8,))],
        compiler_params=pltpu.CompilerParams(vmem_limit_bytes=16 * 1024 * 1024),
        name="deliver",
    )(landed, share)
    return stored.reshape(2 * N_LIST * BLK, D), sums, counts


def solution(mesh):
    both = ("ingest", "list")
    in_specs = (P(both, None), P(both), P(both, None), P(both, None), P("list", None), P())
    out_specs = (P(both, None), P(both, None), P(both, None))
    return jax.shard_map(shards, mesh=mesh, in_specs=in_specs, out_specs=out_specs, check_vma=False)
```

```python
import jax
import jax.numpy as jnp
from jax import lax
from jax.experimental import pallas as pl
from jax.experimental.pallas import tpu as pltpu
from jax.sharding import PartitionSpec as P

M = 96
D = 768
KS = 256
LIST_DEV = 4096
BLK = 256
BDEV = 12
ROWS_DEV = BDEV * BLK
N_LIST = 16
N_INGEST = 8
LANES = 128
CHUNKS = D // LANES
WIDE = D + LANES
HI = 64
MESH = pl.DeviceIdType.MESH
F32 = jnp.float32
BF16 = jnp.bfloat16
FAR = (1, 3, 2)


RAW = ((1, 1), (3, 1), (1, 3), (3, 3))
LATER = ((2, 1), (2, 3), (1, 2), (3, 2), (2, 2))
LAST = ((1, 0), (3, 0), (2, 0), (0, 1), (0, 3), (0, 2))


def iota(shape, axis):
    return lax.broadcasted_iota(jnp.int32, shape, axis)


def exchange(
    vec_hbm, lists, codes_hbm, counts, cent_hbm, rot_hbm,
    landed, mid, share,
    vec, codes, cent, rot, stage, ids_out, ids_in, ids_smem, centre_rows, rows_in, table,
    natural, left, right, left_c, right_c, totals, ring_in, ring_sum, part_out, part_in,
    load_sem, smem_sem, s1, r1, s2, r2, s_ids, r_ids, s_rows, r_rows, s_ring, r_ring, s_part, r_part,
):
    i = lax.axis_index("ingest")
    j = lax.axis_index("list")
    y = j // 4
    z = j % 4

    def at(dy, dz):
        return ((y + dy) % 4) * 4 + (z + dz) % 4

    loads = [
        pltpu.make_async_copy(vec_hbm, vec, load_sem.at[0]),
        pltpu.make_async_copy(cent_hbm, cent, load_sem.at[1]),
        pltpu.make_async_copy(codes_hbm, codes, load_sem.at[2]),
        pltpu.make_async_copy(rot_hbm, rot, load_sem.at[3]),
    ]
    loads[0].start()

    barrier = pltpu.get_barrier_semaphore()
    for o in range(1, N_LIST):
        pl.semaphore_signal(barrier, inc=1, device_id=(i, at(o // 4, o % 4)), device_id_type=MESH)
    for o in range(1, N_INGEST):
        pl.semaphore_signal(barrier, inc=1, device_id=((i + o) % N_INGEST, j), device_id_type=MESH)

    owners = [lists[b] >> 12 for b in range(BDEV)]
    slots = []
    for b in range(BDEV):
        rank = jnp.int32(0)
        for c in range(b):
            rank = rank + jnp.where(owners[c] == owners[b], 1, 0)
        limit = jnp.int32(0)
        for o in range(N_LIST):
            limit = jnp.where(owners[b] == o, counts[0, o], limit)
        slots.append(jnp.where(rank < limit, owners[b] * 2 + rank, -1))
    for b in range(BDEV):
        table[b] = slots[b]

    def source_of(slot):
        block = jnp.int32(0)
        for b in range(1, BDEV):
            block = jnp.where(slots[b] == slot, b, block)
        return block

    def list_of(slot):
        found = jnp.int32(-1)
        for b in range(BDEV):
            found = jnp.where(slots[b] == slot, lists[b] & (LIST_DEV - 1), found)
        return found

    lane8 = iota((8, LANES), 1)
    for o in range(N_LIST):
        owner = at(o // 4, o % 4)
        ids_out[o] = jnp.where(lane8 == 0, list_of(owner * 2), list_of(owner * 2 + 1))
    ids_in[j] = ids_out[0]

    for load in loads[1:]:
        load.start()
    loads[0].wait()

    hops = {}

    def send(place, d, e, r, packed):
        if packed is not None:
            stage[place] = packed
        along = (0, d) if r == 0 else (d, 0)
        if d == 0:
            along = (e, 0) if r == 0 else (0, e)
        if d == 0 or e == 0:
            landing, gone, come = landed.at[j * 2 + r], s2.at[r, d, e], r2.at[r, d, e]
        else:
            landing, gone, come = mid.at[r, d, e], s1.at[r, d, e], r1.at[r, d, e]
        copy = pltpu.make_async_remote_copy(
            src_ref=stage.at[place], dst_ref=landing, send_sem=gone, recv_sem=come,
            device_id=(i, at(*along)), device_id_type=MESH)
        copy.start()
        hops[r, d, e] = copy

    def slot_of(d, e, r):
        return (at(e, d) if r == 0 else at(d, e)) * 2 + r

    def pack_raw(first, pairs):
        for n, (d, e) in enumerate(pairs):
            for r in range(2):
                stage[first + 2 * n + r] = vec[source_of(slot_of(d, e, r))]

    def send_raw(first, pairs):
        for n, (d, e) in enumerate(pairs):
            for r in range(2):
                send(first + 2 * n + r, d, e, r, None)

    pack_raw(0, RAW)
    pl.semaphore_wait(barrier, N_LIST - 1 + N_INGEST - 1)

    id_copies = []
    for o in range(1, N_LIST):
        copy = pltpu.make_async_remote_copy(
            src_ref=ids_out.at[o, pl.ds(0, 1)], dst_ref=ids_in.at[j, pl.ds(0, 1)], send_sem=s_ids.at[o], recv_sem=r_ids.at[o],
            device_id=(i, at(o // 4, o % 4)), device_id_type=MESH)
        copy.start()
        id_copies.append(copy)

    send_raw(0, RAW[:2])

    for copy in id_copies:
        copy.wait_recv()
    to_smem = pltpu.make_async_copy(ids_in, ids_smem, smem_sem.at[0])
    to_smem.start()
    to_smem.wait()
    loads[1].wait()
    sub16 = iota((16, D), 0)
    pad = jnp.zeros((2, LANES), F32)
    row_copies = []
    for o in range(N_LIST):
        source = at(-(o // 4) % 4, -(o % 4) % 4)
        parts = []
        for r in range(2):
            wanted = jnp.maximum(ids_smem[source, 0, r], 0)
            near = cent[wanted >> 4].astype(F32)
            row = jnp.sum(jnp.where(sub16 == (wanted & 15), near, 0.0), axis=0, keepdims=True)
            parts += [row[:, k * LANES:(k + 1) * LANES] for k in range(CHUNKS)] + [pad]
        centre_rows[source] = jnp.concatenate(parts, axis=0).astype(BF16)
        if o == 0:
            rows_in[j] = centre_rows[source]
        else:
            copy = pltpu.make_async_remote_copy(
                src_ref=centre_rows.at[source], dst_ref=rows_in.at[j], send_sem=s_rows.at[o], recv_sem=r_rows.at[o],
                device_id=(i, source), device_id_type=MESH)
            copy.start()
            row_copies.append(copy)

    send_raw(4, RAW[2:])
    loads[2].wait()
    loads[3].wait()
    for copy in row_copies:
        copy.wait_recv()

    eye = (iota((BLK, BLK), 0) == iota((BLK, BLK), 1)).astype(BF16)
    none = jnp.zeros((LANES - M, BLK), F32)

    def rotate(rows, centre):
        residual = jnp.concatenate([
            (rows[:, k * LANES:(k + 1) * LANES].astype(F32) - centre[k:k + 1, :]).astype(BF16) for k in range(CHUNKS)
        ], axis=1)
        return jnp.dot(residual, rot[...], preferred_element_type=F32)

    def encode(b, carry):
        slot = table[b]
        kept = slot >= 0
        slot = jnp.maximum(slot, 0)
        tile = rows_in[slot >> 1].astype(F32)
        centre = jnp.where((slot & 1) == 0, tile[0:8], tile[8:16])
        vec[b] = jnp.where(kept, rotate(vec[b], centre), 0.0).astype(BF16)
        code = codes[:, pl.ds(pl.multiple_of(b * BLK, BLK), BLK)]
        both = jnp.concatenate([
            (code >> 6).astype(F32), none, jnp.where(kept, (code >> 4).astype(F32), -1.0), none], axis=0).astype(BF16)
        natural[b] = lax.dot_general(
            eye, both, (((1,), (1,)), ((), ())), preferred_element_type=F32).astype(BF16)
        return carry

    lax.fori_loop(0, BDEV, encode, 0)

    def encoded(slot):
        filled = jnp.int32(0)
        for b in range(BDEV):
            filled = filled + jnp.where(slots[b] == slot, 1, 0)
        return jnp.where(filled > 0, vec[source_of(slot)], jnp.zeros((BLK, D), BF16))

    place = 8
    def send_encoded(first, pairs):
        for n, (d, e) in enumerate(pairs):
            for r in range(2):
                send(first + 2 * n + r, d, e, r, encoded(slot_of(d, e, r)))

    send_encoded(8, LATER)
    for r in range(2):
        landed[j * 2 + r] = encoded(j * 2 + r)

    totals[:, D:] = jnp.zeros((KS, LANES), F32)
    lane = iota((BLK, LANES), 1)
    upper = (lane >= 64).astype(F32)
    lane_r = iota((HI, 2 * LANES), 1)
    lane_c = iota((HI, LANES), 1)
    lane_16 = iota((16, 2 * LANES), 1)
    hi_rows = iota((HI, BLK), 0)
    wide_row = iota((LANES, 2 * LANES), 0)
    wide_lane = iota((LANES, 2 * LANES), 1)
    digit = (iota((BLK, 2 * LANES), 1) // 16).astype(F32)

    second = {}
    for d, e in RAW + LATER:
        for r in range(2):
            owner = at(e, 0) if r == 0 else at(0, e)
            origin = at(0, -d) if r == 0 else at(-d, 0)
            second[r, d, e] = pltpu.make_async_remote_copy(
                src_ref=mid.at[r, d, e], dst_ref=landed.at[origin * 2 + r], send_sem=s2.at[r, d, e],
                recv_sem=r2.at[r, d, e], device_id=(i, owner), device_id_type=MESH)

    def forward(pairs):
        for d, e in pairs:
            for r in range(2):
                hops[r, d, e].wait_recv()
                second[r, d, e].start()

    def group(g, carry):
        @pl.when(g == 1)
        def early():
            forward(RAW[:2])

        @pl.when(g == 3)
        def next():
            forward(RAW[2:])

        spread = (wide_row == g * 16 + (wide_lane // LANES) * 8 + (wide_lane % 64) // 8).astype(BF16)
        spread_c = (wide_row == g * 16 + wide_lane % 16).astype(BF16)
        cols = pl.ds(pl.multiple_of(g * LANES, LANES), LANES)
        base = pl.multiple_of(g * 16, 16)

        def build(b, inner):
            rows = pl.ds(pl.multiple_of(b * BLK, BLK), BLK)
            lo = jnp.dot(natural[b, :, :LANES], spread, preferred_element_type=F32)
            e = vec[b, :, cols].astype(F32)
            turned = pltpu.roll(e, 64, 1)
            for h in range(2):
                both = jnp.where(lane < 64, e, turned) if h == 0 else jnp.where(lane < 64, turned, e)
                lo_h = lo[:, h * LANES:(h + 1) * LANES]
                for p in range(2):
                    right[h, rows, p * LANES:(p + 1) * LANES] = jnp.where(
                        lo_h == upper + float(2 * p), both, 0.0).astype(BF16)
            high = jnp.dot(natural[b, :, LANES:], spread_c, preferred_element_type=F32)
            right_c[rows, :] = jnp.where(high == digit, 1.0, 0.0).astype(BF16)
            code = codes[pl.ds(base, 16), rows] & 15
            for m in range(16):
                left_c[m * 16:(m + 1) * 16, rows] = jnp.where(
                    code[m:m + 1, :] == hi_rows[:16], 1.0, 0.0).astype(BF16)
            return inner

        lax.fori_loop(0, BDEV, build, 0)
        halves = []
        for h in range(2):

            def build_left(b, inner):
                rows = pl.ds(pl.multiple_of(b * BLK, BLK), BLK)
                code = codes[pl.ds(base + h * 8, 8), rows] & (HI - 1)
                for m in range(8):
                    left[m * HI:(m + 1) * HI, rows] = jnp.where(code[m:m + 1, :] == hi_rows, 1.0, 0.0).astype(BF16)
                return inner

            lax.fori_loop(0, BDEV, build_left, 0)
            sums = jnp.dot(left[...], right[h], preferred_element_type=F32)
            picked = jnp.zeros((HI, 2 * LANES), F32)
            for m in range(8):
                picked = picked + jnp.where((lane_r % 64) // 8 == m, sums[m * HI:(m + 1) * HI, :], 0.0)
            halves.append(picked)
        for p in range(2):
            a = halves[0][:, p * LANES:(p + 1) * LANES]
            c = halves[1][:, p * LANES:(p + 1) * LANES]
            totals[(2 * p) * HI:(2 * p + 1) * HI, cols] = jnp.where(lane_c < 64, a, pltpu.roll(c, 64, 1))
            totals[(2 * p + 1) * HI:(2 * p + 2) * HI, cols] = jnp.where(lane_c < 64, pltpu.roll(a, 64, 1), c)
        found = jnp.dot(left_c[...], right_c[...], preferred_element_type=F32)
        picked = jnp.zeros((16, 2 * LANES), F32)
        for m in range(16):
            picked = picked + jnp.where(lane_16 % 16 == m, found[m * 16:(m + 1) * 16, :], 0.0)
        for q in range(16):
            part = picked[:, (q // 8) * LANES:(q // 8 + 1) * LANES]
            moved = pltpu.roll(part, (g * 16 - (q % 8) * 16) % LANES, 1)
            totals[q * 16:(q + 1) * 16, D:] += jnp.where(lane_c[:16] // 16 == g, moved, 0.0)
        return carry

    lax.fori_loop(0, CHUNKS, group, 0)

    slab = KS // N_INGEST
    ring_copies = []
    for o in range(1, N_INGEST):
        target = (i + o) % N_INGEST
        copy = pltpu.make_async_remote_copy(
            src_ref=totals.at[pl.ds(pl.multiple_of(target * slab, slab), slab), :], dst_ref=ring_in.at[o],
            send_sem=s_ring.at[o], recv_sem=r_ring.at[o], device_id=(target, j), device_id_type=MESH)
        copy.start()
        ring_copies.append(copy)

    send_encoded(18, LAST)

    for copy in ring_copies:
        copy.wait_recv()
    whole = totals[pl.ds(pl.multiple_of(i * slab, slab), slab), :]
    for o in range(1, N_INGEST):
        whole = whole + ring_in[o]
    ring_sum[...] = whole
    zero_row = jnp.zeros((1, LANES), F32)
    for o in range(N_LIST):
        target = at(o // 4, o % 4)
        eight = ring_sum[pl.ds(pl.multiple_of((target // 4) * 8, 8), 8), :]
        rows = []
        for r in range(2):
            row = jnp.sum(jnp.where(iota((8, WIDE), 0) == (target % 4) * 2 + r, eight, 0.0), axis=0, keepdims=True)
            rows += [row[:, k * LANES:(k + 1) * LANES] for k in range(CHUNKS + 1)] + [zero_row]
        part_out[o] = jnp.concatenate(rows, axis=0)
    part_copies = []
    for o in range(1, N_LIST):
        copy = pltpu.make_async_remote_copy(
            src_ref=part_out.at[o], dst_ref=part_in.at[o], send_sem=s_part.at[o], recv_sem=r_part.at[o],
            device_id=(i, at(o // 4, o % 4)), device_id_type=MESH)
        copy.start()
        part_copies.append(copy)

    forward(LATER)

    def finish(slot, r):
        source = slot // 2
        centre = centre_rows[source].astype(F32)[r * 8:(r + 1) * 8]
        rotated = rotate(landed[slot], centre)
        landed[slot] = jnp.where(ids_smem[source, 0, r] >= 0, rotated, 0.0).astype(BF16)

    def arrival(t, carry):
        d, e = 1 + 2 * (t % 2), 1 + 2 * (t // 2)
        for r in range(2):
            origin = at(4 - e, 4 - d) if r == 0 else at(4 - d, 4 - e)
            slot = origin * 2 + r
            pltpu.make_async_remote_copy(
                src_ref=stage.at[0], dst_ref=landed.at[slot], send_sem=s2.at[r, d, e], recv_sem=r2.at[r, d, e],
                device_id=(i, origin), device_id_type=MESH).wait_recv()
            finish(slot, r)
        return carry

    lax.fori_loop(0, 4, arrival, 0)

    for copy in part_copies:
        copy.wait_recv()
    total = part_out[0]
    for o in range(1, N_LIST):
        total = total + part_in[o]
    share[...] = total

    for d, e in LATER + LAST:
        for r in range(2):
            (hops[r, d, e] if d == 0 or e == 0 else second[r, d, e]).wait_recv()
    for copy in id_copies + row_copies + ring_copies + part_copies + list(hops.values()) + list(second.values()):
        copy.wait_send()


def deliver(landed, share, stored, sums, counts, sem):
    parts = [
        pltpu.make_async_copy(landed.at[pl.ds(n * 4, 4)], stored.at[pl.ds(n * 4, 4)], sem.at[n]) for n in range(8)
    ]
    for part in parts:
        part.start()
    for r in range(2):
        for k in range(CHUNKS):
            sums[r:r + 1, k * LANES:(k + 1) * LANES] = share[r * 8 + k:r * 8 + k + 1, :]
        counts[r:r + 1, :] = share[r * 8 + CHUNKS:r * 8 + CHUNKS + 1, :M]
    for part in parts:
        part.wait()


def shards(vectors, list_ids, code_ids, block_counts, centroids, rotation):
    hbm = pl.BlockSpec(memory_space=pl.ANY)
    smem = pl.BlockSpec(memory_space=pltpu.SMEM)
    vmem = pl.BlockSpec(memory_space=pltpu.VMEM)
    dma = pltpu.SemaphoreType.DMA
    landed, _, share = pl.pallas_call(
        exchange,
        out_shape=(
            pltpu.VMEM((2 * N_LIST, BLK, D), BF16),
            jax.ShapeDtypeStruct((2, 4, 4, BLK, D), BF16),
            pltpu.VMEM((16, LANES), F32),
        ),
        in_specs=[hbm, smem, hbm, smem, hbm, hbm],
        out_specs=(vmem, hbm, vmem),
        scratch_shapes=[
            pltpu.VMEM((BDEV, BLK, D), BF16),
            pltpu.VMEM((M, ROWS_DEV), jnp.int32),
            pltpu.VMEM((LIST_DEV // 16, 16, D), BF16),
            pltpu.VMEM((D, D), BF16),
            pltpu.VMEM((2 * N_LIST - 2, BLK, D), BF16),
            pltpu.VMEM((N_LIST, 8, LANES), jnp.int32),
            pltpu.VMEM((N_LIST, 8, LANES), jnp.int32),
            pltpu.SMEM((N_LIST, 8, LANES), jnp.int32),
            pltpu.VMEM((N_LIST, 16, LANES), BF16),
            pltpu.VMEM((N_LIST, 16, LANES), BF16),
            pltpu.SMEM((BDEV,), jnp.int32),
            pltpu.VMEM((BDEV, BLK, 2 * LANES), BF16),
            pltpu.VMEM((8 * HI, ROWS_DEV), BF16),
            pltpu.VMEM((2, ROWS_DEV, 2 * LANES), BF16),
            pltpu.VMEM((2 * LANES, ROWS_DEV), BF16),
            pltpu.VMEM((ROWS_DEV, 2 * LANES), BF16),
            pltpu.VMEM((KS, WIDE), F32),
            pltpu.VMEM((N_INGEST, KS // N_INGEST, WIDE), F32),
            pltpu.VMEM((KS // N_INGEST, WIDE), F32),
            pltpu.VMEM((N_LIST, 16, LANES), F32),
            pltpu.VMEM((N_LIST, 16, LANES), F32),
            dma((4,)), dma((1,)),
            dma((2, 4, 4)), dma((2, 4, 4)), dma((2, 4, 4)), dma((2, 4, 4)),
            dma((N_LIST,)), dma((N_LIST,)), dma((N_LIST,)), dma((N_LIST,)),
            dma((N_INGEST,)), dma((N_INGEST,)), dma((N_LIST,)), dma((N_LIST,)),
        ],
        compiler_params=pltpu.CompilerParams(
            collective_id=1, has_side_effects=True, vmem_limit_bytes=47 * 1024 * 1024),
        name="exchange",
    )(
        vectors.reshape(BDEV, BLK, D), list_ids, code_ids.T, block_counts,
        centroids.reshape(LIST_DEV // 16, 16, D), rotation,
    )
    stored, sums, counts = pl.pallas_call(
        deliver,
        out_shape=(
            jax.ShapeDtypeStruct((2 * N_LIST, BLK, D), BF16),
            jax.ShapeDtypeStruct((2, D), F32),
            jax.ShapeDtypeStruct((2, M), F32),
        ),
        in_specs=[vmem, vmem],
        out_specs=(hbm, vmem, vmem),
        scratch_shapes=[dma((8,))],
        compiler_params=pltpu.CompilerParams(vmem_limit_bytes=16 * 1024 * 1024),
        name="deliver",
    )(landed, share)
    return stored.reshape(2 * N_LIST * BLK, D), sums, counts


def solution(mesh):
    both = ("ingest", "list")
    in_specs = (P(both, None), P(both), P(both, None), P(both, None), P("list", None), P())
    out_specs = (P(both, None), P(both, None), P(both, None))
    return jax.shard_map(shards, mesh=mesh, in_specs=in_specs, out_specs=out_specs, check_vma=False)
```
